128 devices in a mesh: row: 8 (over x, core), col: 16 (over y, z).
Axes of the slice: x: 4, y: 4, z: 4, core: 2. Of those that a mesh axis runs over, the one named last changes fastest.
Arguments:
- modes: float32 [2048, 30720], P('col', 'row'), may hold values from -6 to 6
- prev_modes: float32 [2048, 30720], P('col', 'row'), may hold values from -9 to 9
- first_vectors: float32 [256, 30720], P('col', 'row'), may hold values from -1 to 1, as said below
- first_factor: float32 [256, 256], replicated, may hold values from -0.4 to 0.6, as said below
- second_vectors: float32 [256, 30720], P('col', 'row'), may hold values from -1 to 1, as said below
- second_factor: float32 [256, 256], replicated, may hold values from -0.4 to 0.6, as said below
Outputs:
- moved: float32 [2048, 30720], P('col', 'row')
- correlation: float32 [2048, 2048], P('col', 'row')
The draws below stay inside these ranges and needn't reach their ends.
Inputs may be any that keep to these rules, and one draw needn't show every extreme that they name: `first_vectors`: zero where the column index is below the row index, one where they are equal. `second_vectors`: zero where the column index is below the row index plus 256, one where it equals it. `first_factor`: upper triangular. `second_factor`: upper triangular.
All inputs are finite; a program needn't handle non-finite values.
Results may differ from the reference program's by a relative error of at most 0.00005.
Values sent between devices are 32-bit elements; how exact they have to be, the bound alone decides.
A program may use at most 128 MiB of HBM per device.

```python
import jax
import jax.numpy as jnp
from jax import lax

N = 30720
K = 2048
PANEL = 256


def common_draw(key):
    return jnp.clip(jax.random.normal(key, (K, N), jnp.float32), -6.0, 6.0)


def draw_modes(key, part):
    base = common_draw(key)
    return base


def draw_prev_modes(key, part):
    base = common_draw(key)
    key = jax.random.fold_in(key, 12)
    noise = jnp.clip(jax.random.normal(key, (K, N), jnp.float32), -6.0, 6.0)
    return 0.8 * base + 0.6 * noise


def build_vectors(values, offset):
    panel_ids = jnp.arange(PANEL, dtype=jnp.int32)[:, None] + offset
    entry_ids = jnp.arange(N, dtype=jnp.int32)[None, :]
    ones = jnp.ones((PANEL, N), jnp.float32)
    zeros = jnp.zeros((PANEL, N), jnp.float32)
    return jnp.where(entry_ids == panel_ids, ones, jnp.where(entry_ids > panel_ids, values, zeros))


def vector_values(key, spread):
    return jnp.clip(jax.random.normal(key, (PANEL, N), jnp.float32), -6.0, 6.0) * (spread / N ** 0.5)


def draw_first_vectors(key, part):
    key = jax.random.fold_in(key, 21)
    values = vector_values(key, 2.0)
    return build_vectors(values, 0)


def draw_second_vectors(key, part):
    key = jax.random.fold_in(key, 22)
    values = vector_values(key, 2.0)
    return build_vectors(values, PANEL)


def build_factor(diagonal, upper):
    row_ids = jnp.arange(PANEL, dtype=jnp.int32)[:, None]
    col_ids = jnp.arange(PANEL, dtype=jnp.int32)[None, :]
    zeros = jnp.zeros((PANEL, PANEL), jnp.float32)
    return jnp.where(row_ids == col_ids, diagonal, jnp.where(row_ids < col_ids, upper, zeros))


def draw_first_factor(key, part):
    key = jax.random.fold_in(key, 31)
    first_key, second_key = jax.random.split(key)
    diagonal = 0.25 * jnp.exp(jax.random.uniform(first_key, (PANEL, PANEL), jnp.float32) * 0.78)
    upper = jnp.clip(jax.random.normal(second_key, (PANEL, PANEL), jnp.float32), -6.0, 6.0) * 0.05
    return build_factor(diagonal, upper)


def draw_second_factor(key, part):
    key = jax.random.fold_in(key, 32)
    first_key, second_key = jax.random.split(key)
    diagonal = 0.25 * jnp.exp(jax.random.uniform(first_key, (PANEL, PANEL), jnp.float32) * 0.78)
    upper = jnp.clip(jax.random.normal(second_key, (PANEL, PANEL), jnp.float32), -6.0, 6.0) * 0.05
    return build_factor(diagonal, upper)


def setup_inputs(seed: int = 0) -> dict:
    splits = jax.random.split(jax.random.key(seed), 7)
    modes = draw_modes(jax.random.fold_in(splits[6], 71), 0)
    prev_modes = draw_prev_modes(jax.random.fold_in(splits[6], 71), 0)
    first_vectors = draw_first_vectors(jax.random.fold_in(splits[6], 71), 0)
    first_factor = draw_first_factor(jax.random.fold_in(splits[6], 71), 0)
    second_vectors = draw_second_vectors(jax.random.fold_in(splits[6], 71), 0)
    second_factor = draw_second_factor(jax.random.fold_in(splits[6], 71), 0)
    return dict(modes=modes, prev_modes=prev_modes, first_vectors=first_vectors, first_factor=first_factor, second_vectors=second_vectors, second_factor=second_factor)


def reflect_panel(vectors, factor, target):
    highest = lax.Precision.HIGHEST
    projected = jnp.dot(vectors, target.T, precision=highest)
    scaled = jnp.dot(factor, projected, precision=highest)
    return target - jnp.dot(scaled.T, vectors, precision=highest)


def reference(modes, prev_modes, first_vectors, first_factor, second_vectors, second_factor):
    partly = reflect_panel(second_vectors, second_factor, modes)
    moved = reflect_panel(first_vectors, first_factor, partly)
    correlation = jnp.dot(moved, prev_modes.T, precision=lax.Precision.HIGHEST) / N
    return moved, correlation
```

```python
import functools

import jax
import jax.numpy as jnp
from jax import lax
from jax.experimental import pallas as pl
from jax.experimental.pallas import tpu as pltpu
from jax.sharding import PartitionSpec as P

N = 30720
MESH = pl.DeviceIdType.MESH
F32 = jnp.float32
BF16 = jnp.bfloat16
W = 1024
ODD_FIRST = (1, 3, 2)


def split(value):
    high = value.astype(BF16)
    return high, (value - high.astype(F32)).astype(BF16)


def dot3(left, right, dims):
    (lh, ll), (rh, rl) = left, right
    mul = functools.partial(lax.dot_general, dimension_numbers=(dims, ((), ())), preferred_element_type=F32)
    return mul(lh, rh) + (mul(lh, rl) + mul(ll, rh))


NT = ((1,), (1,))
NN = ((1,), (0,))


class Names:
    def __init__(self):
        self.ids = {}

    def __call__(self, *name):
        return self.ids.setdefault(name, len(self.ids))


def kernel(m_in, p_in, v1_in, v2_in, f1, f2, out_m, out_c,
           mk, pk, vk, mh, ml, vh, vl, ph, plo, at, ac, ax, asum, ay, af, wh, wl,
           ck, cs, cc, cx, cf, cy, ss, rs, ls):
    r, col = lax.axis_index("row"), lax.axis_index("col")
    x, c = lax.div(r, 2), lax.rem(r, 2)
    y, z = lax.div(col, 4), lax.rem(col, 4)
    eight = lax.rem(y + c, 2) == 0

    def wrap(a):
        return lax.rem(a, 4)

    def yid(d):
        return (r, wrap(y + d) * 4 + z)

    def zid(d):
        return (r, y * 4 + wrap(z + d))

    def xid(d):
        return (wrap(x + d) * 2 + c, col)

    other = (x * 2 + 1 - c, col)
    names, local_names = Names(), Names()

    def both(fn):
        @pl.when(eight)
        def _():
            fn(8)

        @pl.when(jnp.logical_not(eight))
        def _():
            fn(7)

    def remote(name, src, dst, dev):
        i = names(*name)
        return pltpu.make_async_remote_copy(
            src_ref=src, dst_ref=dst, send_sem=ss.at[i], recv_sem=rs.at[i], device_id=dev, device_id_type=MESH)

    def quarter(q, n):
        start = 15 * lax.div(q, 2) + lax.rem(q, 2) * (8 - c)
        return pl.ds(pl.multiple_of(start * 128, 128), n * 128)

    def width(n, d):
        return 15 - n if d % 2 else n

    def prow(yy, zz, half=None):
        base = (yy * 4 + zz) * 128
        if half is None:
            return pl.ds(pl.multiple_of(base, 128), 128)
        return pl.ds(pl.multiple_of(base + half * 64, 64), 64)

    def mrow(yy):
        return pl.ds(pl.multiple_of(yy * 128, 128), 128)

    sends = []

    def y_v(n, d, p):
        nd, q = width(n, d), wrap(y + d)
        src = (v1_in, v2_in)[p]
        return remote(("yv", d, p), src.at[:, quarter(q, nd)], vk.at[p, y, z, :, pl.ds(0, nd * 128)], yid(d))

    def y_v_in(n, d, p):
        dst = vk.at[p, wrap(y + 4 - d), z, :, pl.ds(0, n * 128)]
        return remote(("yv", d, p), dst, dst, yid(d))

    def y_m(n, d):
        nd, q = width(n, d), wrap(y + d)
        return remote(("ym", d), m_in.at[:, quarter(q, nd)], mk.at[mrow(y), pl.ds(0, nd * 128)], yid(d))

    def y_m_in(n, d):
        dst = mk.at[mrow(wrap(y + 4 - d)), pl.ds(0, n * 128)]
        return remote(("ym", d), dst, dst, yid(d))

    def y_p(n, d, half):
        nd, q = width(n, d), wrap(y + d)
        return remote(("yp", d, half), p_in.at[pl.ds(half * 64, 64), quarter(q, nd)],
                      pk.at[prow(y, z, half), pl.ds(0, nd * 128)], yid(d))

    def y_p_in(n, d, half):
        dst = pk.at[prow(wrap(y + 4 - d), z, half), pl.ds(0, n * 128)]
        return remote(("yp", d, half), dst, dst, yid(d))

    def z_v(n, s):
        ref = vk.at[:, :, z, :, pl.ds(0, n * 128)]
        return remote(("zv", s), ref, ref, zid(s))

    def z_v_in(n, s):
        ref = vk.at[:, :, wrap(z + 4 - s), :, pl.ds(0, n * 128)]
        return remote(("zv", s), ref, ref, zid(s))

    def z_vf(n, s):
        ref = vk.at[0 if s == 1 else 1, :, wrap(z + 4 - s), :, pl.ds(0, n * 128)]
        return remote(("zvf", s), ref, ref, zid(s))

    def z_vf_in(n, s):
        ref = vk.at[0 if s == 1 else 1, :, wrap(z + 2), :, pl.ds(0, n * 128)]
        return remote(("zvf", s), ref, ref, zid(s))

    def z_p(n, e, s, half):
        ref = pk.at[prow(wrap(y + e), z, half), pl.ds(0, n * 128)]
        src = p_in.at[pl.ds(half * 64, 64), quarter(y, n)] if e == 0 else ref
        return remote(("zp", e, s, half), src, ref, zid(s))

    def z_p_in(n, e, s, half):
        ref = pk.at[prow(wrap(y + e), wrap(z + 4 - s), half), pl.ds(0, n * 128)]
        return remote(("zp", e, s, half), ref, ref, zid(s))

    def z_pf(n, e, s):
        ref = pk.at[prow(wrap(y + e), wrap(z + 4 - s), 0 if s == 1 else 1), pl.ds(0, n * 128)]
        return remote(("zpf", e, s), ref, ref, zid(s))

    def z_pf_in(n, e, s):
        ref = pk.at[prow(wrap(y + e), wrap(z + 2), 0 if s == 1 else 1), pl.ds(0, n * 128)]
        return remote(("zpf", e, s), ref, ref, zid(s))

    def y_r(n, d):
        q = wrap(y + d)
        return remote(("yr", d), mk.at[mrow(q), pl.ds(0, n * 128)], out_m.at[:, quarter(y, n)], yid(d))

    def y_r_in(n, d):
        dst = out_m.at[:, quarter(wrap(y + 4 - d), width(n, d))]
        return remote(("yr", d), dst, dst, yid(d))

    def start(*fns):
        both(lambda n: [f(n).start() for f in fns] and None)
        sends.extend(fns)

    def arrived(*fns):
        both(lambda n: [f(n).wait_recv() for f in fns] and None)

    part = functools.partial

    @pl.when(jnp.logical_not(eight))
    def _():
        mk[:, pl.ds(896, 128)] = jnp.zeros((512, 128), F32)
        pk[:, pl.ds(896, 128)] = jnp.zeros((2048, 128), F32)
        vk[:, :, :, :, pl.ds(896, 128)] = jnp.zeros((2, 4, 4, 16, 128), F32)

    barrier = pltpu.get_barrier_semaphore()
    peers = [yid(1), yid(2), yid(3), zid(1), zid(3), xid(1), xid(2), xid(3), other]
    for dev in peers:
        pl.semaphore_signal(barrier, inc=1, device_id=dev, device_id_type=MESH)
    pl.semaphore_wait(barrier, len(peers))

    start(*[part(y_v, d=d, p=p) for d in ODD_FIRST for p in (0, 1)])
    start(part(z_p, e=0, s=1, half=0), part(z_p, e=0, s=3, half=1))

    def own(n):
        return [
            pltpu.make_async_copy(v1_in.at[:, quarter(y, n)], vk.at[0, y, z, :, pl.ds(0, n * 128)], ls.at[0]),
            pltpu.make_async_copy(v2_in.at[:, quarter(y, n)], vk.at[1, y, z, :, pl.ds(0, n * 128)], ls.at[1]),
            pltpu.make_async_copy(m_in.at[:, quarter(y, n)], mk.at[mrow(y), pl.ds(0, n * 128)], ls.at[2]),
            pltpu.make_async_copy(p_in.at[:, quarter(y, n)], pk.at[prow(y, z), pl.ds(0, n * 128)], ls.at[3]),
        ]

    both(lambda n: [q.start() for q in own(n)] and None)
    start(*[part(y_m, d=d) for d in ODD_FIRST])
    start(*[part(y_p, d=d, half=h) for ds in ((1, 3), (2,)) for h in (0, 1) for d in ds])

    arrived(*[part(y_v_in, d=d, p=p) for d in ODD_FIRST for p in (0, 1)])
    both(lambda n: [q.wait() for q in own(n)] and None)
    start(part(z_v, s=1), part(z_v, s=3))
    start(part(z_p, e=0, s=1, half=1), part(z_p, e=0, s=3, half=0))

    def forward(e):
        arrived(part(z_p_in, e=e, s=1, half=0))
        start(part(z_pf, e=e, s=1))
        arrived(part(z_p_in, e=e, s=3, half=1))
        start(part(z_pf, e=e, s=3))

    def along_z(e, half):
        arrived(part(y_p_in, d=4 - e, half=half))
        order = (1, 3) if half == 0 else (3, 1)
        start(*[part(z_p, e=e, s=s, half=half) for s in order])

    forward(0)
    arrived(part(z_v_in, s=1))
    start(part(z_vf, s=1))
    arrived(part(z_v_in, s=3))
    start(part(z_vf, s=3))

    arrived(*[part(y_m_in, d=d) for d in ODD_FIRST])

    @pl.loop(0, 8)
    def _(i):
        rows = pl.ds(pl.multiple_of(i * 64, 64), 64)
        mh[rows, :], ml[rows, :] = split(mk[rows, :])

    arrived(part(z_vf_in, s=1), part(z_vf_in, s=3))

    @pl.loop(0, 8)
    def _(i):
        p, yy = lax.div(i, 4), lax.rem(i, 4)
        rows = pl.ds(pl.multiple_of(i * 64, 64), 64)
        vh[rows, :], vl[rows, :] = split(vk[p, yy].reshape(64, W))

    @pl.loop(0, 2)
    def _(t):
        rows = pl.ds(pl.multiple_of(t * 256, 256), 256)
        for j in (0, 1):
            cols = pl.ds(j * 256, 256)
            res = dot3((mh[rows, :], ml[rows, :]), (vh[cols, :], vl[cols, :]), NT)
            at[pl.ds(t * 4, 4), pl.ds(0, 64), cols] = res.reshape(4, 64, 256)

    first, second = pl.ds(0, 256), pl.ds(256, 256)
    gram = dot3((vh[first, :], vl[first, :]), (vh[second, :], vl[second, :]), NT)
    at[:, pl.ds(64, 16), first] = gram[:128].reshape(8, 16, 256)
    at[:, pl.ds(64, 16), second] = gram[128:].reshape(8, 16, 256)

    mine, theirs = pl.ds(c * 4, 4), pl.ds((1 - c) * 4, 4)
    fixed = []

    def go(copy):
        copy.start()
        fixed.append(copy)
        return copy

    core_sum = go(remote(("ac",), at.at[theirs], ac, other))
    along_z(1, 0)
    along_z(3, 0)
    core_sum.wait_recv()
    for k in range(4):
        at[c * 4 + k] = at[c * 4 + k] + ac[k]
    x_sum = [go(remote(("ax", d), at.at[c * 4 + wrap(x + d)], ax.at[d - 1], xid(d))) for d in ODD_FIRST]
    along_z(1, 1)
    along_z(3, 1)
    for q in x_sum:
        q.wait_recv()
    asum[...] = (at[c * 4 + x] + ax[0]) + (ax[1] + ax[2])
    y_sum = [go(remote(("ay", d), asum, ay.at[d - 1], yid(d))) for d in ODD_FIRST]
    forward(1)
    along_z(2, 0)
    along_z(2, 1)
    forward(3)
    for q in y_sum:
        q.wait_recv()
    g = c * 4 + x
    af[g] = (asum[...] + ay[0]) + (ay[1] + ay[2])
    x_all = [go(remote(("bx", d), af.at[g], af.at[g], xid(d))) for d in ODD_FIRST]
    for d in ODD_FIRST:
        gd = c * 4 + wrap(x + 4 - d)
        remote(("bx", d), af.at[gd], af.at[gd], xid(d)).wait_recv()
    go(remote(("bc",), af.at[mine], af.at[mine], other))
    remote(("bc",), af.at[theirs], af.at[theirs], other).wait_recv()

    gram = jnp.concatenate([af[:, pl.ds(64, 16), first].reshape(128, 256),
                            af[:, pl.ds(64, 16), second].reshape(128, 256)], axis=0)
    gram2, f1s, f2s = split(gram), split(f1[...]), split(f2[...])
    for t in (0, 1):
        rows = pl.ds(t * 256, 256)
        a1 = af[pl.ds(t * 4, 4), pl.ds(0, 64), first].reshape(256, 256)
        a2 = af[pl.ds(t * 4, 4), pl.ds(0, 64), second].reshape(256, 256)
        w2 = split(dot3(split(a2), f2s, NT))
        wh[rows, second], wl[rows, second] = w2
        w1 = split(dot3(split(a1 - dot3(w2, gram2, NT)), f1s, NT))
        wh[rows, first], wl[rows, first] = w1

    @pl.loop(0, 4)
    def _(j):
        cols = pl.ds(pl.multiple_of(j * 256, 256), 256)
        for t in (0, 1):
            rows = pl.ds(t * 256, 256)
            new = mk[rows, cols] - dot3((wh[rows, :], wl[rows, :]), (vh[:, cols], vl[:, cols]), NN)
            mk[rows, cols] = new
            mh[rows, cols], ml[rows, cols] = split(new)

    start(*[part(y_r, d=d) for d in ODD_FIRST])

    def own_r(n):
        return pltpu.make_async_copy(mk.at[mrow(y), pl.ds(0, n * 128)], out_m.at[:, quarter(y, n)], ls.at[4])

    both(lambda n: own_r(n).start())

    def unit(yy, pair, dst):
        base = pl.multiple_of((yy * 4 + pair * 2) * 128, 256)

        @pl.loop(0, 4)
        def _(i):
            rows = pl.ds(pl.multiple_of(i * 64, 64), 64)
            ph[rows, :], plo[rows, :] = split(pk[pl.ds(pl.multiple_of(base + i * 64, 64), 64), :])

        @pl.loop(0, 2)
        def _(t):
            rows = pl.ds(pl.multiple_of(t * 256, 256), 256)
            dst[yy, rows, :] = dot3((mh[rows, :], ml[rows, :]), (ph[...], plo[...]), NT)

    def to_x(yy, d, wait):
        e = wrap(yy - x + 4)

        @pl.when(e > 0)
        def _():
            i, j = names("cx", d), names("cxr", 1)
            names("cxr", 2), names("cxr", 3)
            copy = pltpu.make_async_remote_copy(
                src_ref=ck.at[yy], dst_ref=cx.at[e - 1], send_sem=ss.at[i], recv_sem=rs.at[j + e - 1],
                device_id=(yy * 2 + c, col), device_id_type=MESH)
            copy.wait_send() if wait else copy.start()

    def reduced(e):
        yy = wrap(y + e)
        remote(("cc", e), cc.at[yy], cc.at[yy], other).wait_recv()

        @pl.loop(0, 4)
        def _(i):
            rows = pl.ds(pl.multiple_of(i * 128, 128), 128)
            ck[yy, rows, :] = ck[yy, rows, :] + cc[yy, rows, :]

        to_x(yy, e, False)

    last = None
    for e in (0, 1, 3, 2):
        yy = wrap(y + e)
        if e == 2:
            forward(2)
        arrived(part(z_p_in, e=e, s=1, half=1), part(z_p_in, e=e, s=3, half=0),
                part(z_pf_in, e=e, s=1), part(z_pf_in, e=e, s=3))
        unit(yy, 1 - c, cs)
        go(remote(("cc", e), cs.at[yy], cc.at[yy], other))
        if last is not None:
            reduced(last)
        unit(yy, c, ck)
        last = e
    reduced(last)

    base = names("cxr", 1)
    for d in range(3):
        pltpu.make_async_remote_copy(
            src_ref=cx.at[d], dst_ref=cx.at[d], send_sem=ss.at[base + d], recv_sem=rs.at[base + d],
            device_id=xid(1), device_id_type=MESH).wait_recv()

    @pl.loop(0, 4)
    def _(i):
        rows = pl.ds(pl.multiple_of(i * 128, 128), 128)
        cf[rows, :] = (ck[x, rows, :] + cx[0, rows, :]) + (cx[1, rows, :] + cx[2, rows, :])

    for d in ODD_FIRST:
        go(remote(("cy", d), cf.at[mrow(wrap(y + d))], cy.at[d - 1], yid(d)))
    for d in ODD_FIRST:
        remote(("cy", d), cf.at[mrow(y)], cy.at[d - 1], yid(d)).wait_recv()
    out_c[...] = ((cf[mrow(y), :] + cy[0]) + (cy[1] + cy[2])) / N

    arrived(*[part(y_r_in, d=d) for d in ODD_FIRST])
    both(lambda n: own_r(n).wait())
    both(lambda n: [f(n).wait_send() for f in sends] and None)
    for copy in fixed:
        copy.wait_send()
    for e in (0, 1, 3, 2):
        to_x(wrap(y + e), e, True)
    assert len(names.ids) <= SEMS


SEMS = 96


def shards(modes, prev_modes, first_vectors, first_factor, second_vectors, second_factor):
    any_, vmem = pl.BlockSpec(memory_space=pl.ANY), pl.BlockSpec(memory_space=pltpu.VMEM)
    V = pltpu.VMEM
    dma = pltpu.SemaphoreType.DMA
    return pl.pallas_call(
        kernel,
        out_shape=(jax.ShapeDtypeStruct((128, 3840), F32), jax.ShapeDtypeStruct((128, 256), F32)),
        in_specs=[any_, any_, any_, any_, vmem, vmem],
        out_specs=(any_, vmem),
        scratch_shapes=[
            V((512, W), F32), V((2048, W), F32), V((2, 4, 4, 16, W), F32),
            V((512, W), BF16), V((512, W), BF16), V((512, W), BF16), V((512, W), BF16),
            V((256, W), BF16), V((256, W), BF16),
            V((8, 80, 512), F32), V((4, 80, 512), F32), V((3, 80, 512), F32), V((80, 512), F32),
            V((3, 80, 512), F32), V((8, 80, 512), F32), V((512, 512), BF16), V((512, 512), BF16),
            V((4, 512, 256), F32), V((4, 512, 256), F32), V((4, 512, 256), F32), V((3, 512, 256), F32),
            V((512, 256), F32), V((3, 128, 256), F32),
            dma((SEMS,)), dma((SEMS,)), dma((5,)),
        ],
        compiler_params=pltpu.CompilerParams(
            collective_id=0, has_side_effects=True, vmem_limit_bytes=56 * 2**20),
        name="reflect_and_correlate",
    )(modes, prev_modes, first_vectors, second_vectors, first_factor, second_factor)


def solution(mesh):
    in_specs = (P("col", "row"), P("col", "row"), P("col", "row"), P(), P("col", "row"), P())
    out_specs = (P("col", "row"), P("col", "row"))
    return jax.shard_map(shards, mesh=mesh, in_specs=in_specs, out_specs=out_specs, check_vma=False)
```

```python
import functools

import jax
import jax.numpy as jnp
from jax import lax
from jax.experimental import pallas as pl
from jax.experimental.pallas import tpu as pltpu
from jax.sharding import PartitionSpec as P

N = 30720
MESH = pl.DeviceIdType.MESH
F32 = jnp.float32
BF16 = jnp.bfloat16
W = 1024
ODD_FIRST = (1, 3, 2)


def split(value):
    high = value.astype(BF16)
    return high, (value - high.astype(F32)).astype(BF16)


def dot3(left, right, dims):
    (lh, ll), (rh, rl) = left, right
    mul = functools.partial(lax.dot_general, dimension_numbers=(dims, ((), ())), preferred_element_type=F32)
    return mul(lh, rh) + (mul(lh, rl) + mul(ll, rh))


NT = ((1,), (1,))
NN = ((1,), (0,))


class Names:
    def __init__(self):
        self.ids = {}

    def __call__(self, *name):
        return self.ids.setdefault(name, len(self.ids))


def kernel(m_in, p_in, v1_in, v2_in, f1, f2, out_m, out_c,
           mk, mp, mv, pk, vk, rh, rl, ph, plo, at, ac, ax, ay, bx_, by_, as_, af, wh, wl,
           ct, cc, cb, kc, kb, cx, bx, sc, sb, fc, fb, dt, cy, of, ss, rs, ls):
    r, col = lax.axis_index("row"), lax.axis_index("col")
    x, c = lax.div(r, 2), lax.rem(r, 2)
    y, z = lax.div(col, 4), lax.rem(col, 4)
    eight = lax.rem(y + c, 2) == 0
    home = c == lax.div(z, 2)
    zl = lax.rem(z, 2)

    def wrap(a):
        return lax.rem(a, 4)

    def yid(d):
        return (r, wrap(y + d) * 4 + z)

    def zid(d):
        return (r, y * 4 + wrap(z + d))

    def xid(d):
        return (wrap(x + d) * 2 + c, col)

    other = (x * 2 + 1 - c, col)
    p_mate = (r, y * 4 + z + 1 - 2 * zl)
    m_mate = (r, y * 4 + 3 - z)
    swap_mate = (x * 2 + 1 - c, y * 4 + 3 - z)
    names = Names()

    def both(fn):
        @pl.when(eight)
        def _():
            fn(8)

        @pl.when(jnp.logical_not(eight))
        def _():
            fn(7)

    def remote(name, src, dst, dev):
        i = names(*name)
        return pltpu.make_async_remote_copy(
            src_ref=src, dst_ref=dst, send_sem=ss.at[i], recv_sem=rs.at[i], device_id=dev, device_id_type=MESH)

    def quarter(q, n):
        start = 15 * lax.div(q, 2) + lax.rem(q, 2) * (8 - c)
        return pl.ds(pl.multiple_of(start * 128, 128), n * 128)

    def width(n, d):
        return 15 - n if d % 2 else n

    def mrow(yy, first=0, count=128):
        return pl.ds(pl.multiple_of(yy * 128 + first, 32), count)

    def lanes(i, step):
        return pl.ds(pl.multiple_of(i * step, step), step)

    sends = []
    fixed = []
    home_sends, away_sends = [], []

    def y_v(n, d, p):
        nd, q = width(n, d), wrap(y + d)
        src = (v1_in, v2_in)[p]
        return remote(("yv", d, p), src.at[:, quarter(q, nd)], vk.at[p, y, z, :, pl.ds(0, nd * 128)], yid(d))

    def y_v_in(n, d, p):
        dst = vk.at[p, wrap(y + 4 - d), z, :, pl.ds(0, n * 128)]
        return remote(("yv", d, p), dst, dst, yid(d))

    def y_m(n, d):
        nd, q = width(n, d), wrap(y + d)
        return remote(("ym", d), m_in.at[:, quarter(q, nd)], mk.at[mrow(y), pl.ds(0, nd * 128)], yid(d))

    def y_m_in(n, d):
        dst = mk.at[mrow(wrap(y + 4 - d)), pl.ds(0, n * 128)]
        return remote(("ym", d), dst, dst, yid(d))

    def y_p(n, d, h):
        nd, q = width(n, d), wrap(y + d)
        return remote(("yp", d, h), p_in.at[h, :, quarter(q, nd)], pk.at[h, 4 - d, zl, :, pl.ds(0, nd * 128)], yid(d))

    def y_p_in(n, d, h):
        dst = pk.at[h, 4 - d, zl, :, pl.ds(0, n * 128)]
        return remote(("yp", d, h), dst, dst, yid(d))

    def z_v(n, s, p):
        ref = vk.at[p, :, z, :, pl.ds(0, n * 128)]
        return remote(("zv", s, p), ref, ref, zid(s))

    def z_v_in(n, s, p):
        ref = vk.at[p, :, wrap(z + 4 - s), :, pl.ds(0, n * 128)]
        return remote(("zv", s, p), ref, ref, zid(s))

    def z_vf(n, s):
        ref = vk.at[0 if s == 1 else 1, :, wrap(z + 4 - s), :, pl.ds(0, n * 128)]
        return remote(("zvf", s), ref, ref, zid(s))

    def z_vf_in(n, s):
        ref = vk.at[0 if s == 1 else 1, :, wrap(z + 2), :, pl.ds(0, n * 128)]
        return remote(("zvf", s), ref, ref, zid(s))

    def z_m0(n, k):
        a, b = ((0, 96), (96, 32))[k]
        return remote(("zm0", k), m_in.at[pl.ds(a, b), quarter(y, n)], mp.at[mrow(y, a, b), pl.ds(0, n * 128)], m_mate)

    def z_m0_in(n, k):
        a, b = ((0, 96), (96, 32))[k]
        ref = mp.at[mrow(y, a, b), pl.ds(0, n * 128)]
        return remote(("zm0", k), ref, ref, m_mate)

    def z_m(n, e):
        rows = mrow(wrap(y + e))
        return remote(("zm", e), mk.at[rows, pl.ds(0, n * 128)], mp.at[rows, pl.ds(0, n * 128)], m_mate)

    def z_p0(n, k):
        a, b = ((0, 3), (3, 1))[k]
        return remote(("zp0", k), p_in.at[pl.ds(a, b), :, quarter(y, n)],
                      pk.at[pl.ds(a, b), 0, zl, :, pl.ds(0, n * 128)], p_mate)

    def z_p0_in(n, k):
        a, b = ((0, 3), (3, 1))[k]
        ref = pk.at[pl.ds(a, b), 0, 1 - zl, :, pl.ds(0, n * 128)]
        return remote(("zp0", k), ref, ref, p_mate)

    def z_p(n, h):
        ref = pk.at[h, pl.ds(1, 3), zl, :, pl.ds(0, n * 128)]
        return remote(("zp", h), ref, ref, p_mate)

    def z_p_in(n, h):
        ref = pk.at[h, pl.ds(1, 3), 1 - zl, :, pl.ds(0, n * 128)]
        return remote(("zp", h), ref, ref, p_mate)

    def y_r(n, d, half):
        return remote(("yr", d, half), mv.at[mrow(wrap(y + d), half * 64, 64), pl.ds(0, n * 128)],
                      out_m.at[pl.ds(half * 64, 64), quarter(y, n)], yid(d))

    def y_r_in(n, d, half):
        dst = out_m.at[pl.ds(half * 64, 64), quarter(wrap(y + 4 - d), width(n, d))]
        return remote(("yr", d, half), dst, dst, yid(d))

    def start(*fns):
        both(lambda n: [f(n).start() for f in fns] and None)
        sends.extend(fns)

    def arrived(*fns):
        both(lambda n: [f(n).wait_recv() for f in fns] and None)

    def go(copy):
        copy.start()
        fixed.append(copy)
        return copy

    part = functools.partial

    @pl.when(jnp.logical_not(eight))
    def _():
        pad = pl.ds(896, 128)
        mk[:, pad] = jnp.zeros((512, 128), F32)
        mp[:, pad] = jnp.zeros((512, 128), F32)
        pk[:, :, :, :, pad] = jnp.zeros((4, 4, 2, 32, 128), F32)
        vk[:, :, :, :, pad] = jnp.zeros((2, 4, 4, 16, 128), F32)

    barrier = pltpu.get_barrier_semaphore()
    peers = [yid(1), yid(2), yid(3), zid(1), zid(3), xid(1), xid(2), xid(3), other, swap_mate]
    for dev in peers:
        pl.semaphore_signal(barrier, inc=1, device_id=dev, device_id_type=MESH)
    pl.semaphore_wait(barrier, len(peers))

    start(*[part(y_v, d=d, p=p) for d in ODD_FIRST for p in (0, 1)])
    start(part(z_p0, k=0), part(z_m0, k=0))

    def own(n):
        return [
            pltpu.make_async_copy(v1_in.at[:, quarter(y, n)], vk.at[0, y, z, :, pl.ds(0, n * 128)], ls.at[0]),
            pltpu.make_async_copy(v2_in.at[:, quarter(y, n)], vk.at[1, y, z, :, pl.ds(0, n * 128)], ls.at[1]),
            pltpu.make_async_copy(m_in.at[:, quarter(y, n)], mk.at[mrow(y), pl.ds(0, n * 128)], ls.at[2]),
            pltpu.make_async_copy(p_in.at[:, :, quarter(y, n)], pk.at[:, 0, zl, :, pl.ds(0, n * 128)], ls.at[3]),
        ]

    both(lambda n: [q.start() for q in own(n)] and None)
    start(*[part(y_m, d=d) for d in ODD_FIRST])

    def y_panel(h):
        start(*[part(y_p, d=d, h=h) for d in ODD_FIRST])

    def z_panel(h):
        arrived(*[part(y_p_in, d=d, h=h) for d in ODD_FIRST])
        start(part(z_p, h=h))

    y_panel(0)
    y_panel(1)

    arrived(*[part(y_v_in, d=d, p=p) for d in ODD_FIRST for p in (0, 1)])
    both(lambda n: [q.wait() for q in own(n)] and None)
    start(part(z_v, s=1, p=0), part(z_v, s=3, p=1), part(z_v, s=1, p=1), part(z_v, s=3, p=0))
    arrived(part(z_v_in, s=1, p=0))
    start(part(z_vf, s=1))
    arrived(part(z_v_in, s=3, p=1))
    start(part(z_vf, s=3))
    start(part(z_p0, k=1), part(z_m0, k=1))
    for e in (1, 3, 2):
        arrived(part(y_m_in, d=4 - e))
        start(part(z_m, e=e))

    @pl.loop(0, 8)
    def _(i):
        rows = pl.ds(pl.multiple_of(i * 64, 64), 64)
        rh[rows, :], rl[rows, :] = split(mk[rows, :])

    arrived(part(z_v_in, s=1, p=1), part(z_v_in, s=3, p=0), part(z_vf_in, s=1), part(z_vf_in, s=3))

    @pl.loop(0, 8)
    def _(i):
        p, yy = lax.div(i, 4), lax.rem(i, 4)
        rows = pl.ds(pl.multiple_of(1024 + i * 64, 64), 64)
        rh[rows, :], rl[rows, :] = split(vk[p, yy].reshape(64, W))

    first, second = pl.ds(0, 256), pl.ds(256, 256)

    @pl.loop(0, 2)
    def _(t):
        rows = pl.ds(pl.multiple_of(t * 256, 256), 256)
        for j, cols in ((0, first), (1, second)):
            vrows = pl.ds(1024 + j * 256, 256)
            res = dot3((rh[rows, :], rl[rows, :]), (rh[vrows, :], rl[vrows, :]), NT)
            at[pl.ds(t * 8, 8), pl.ds(0, 32), cols] = res.reshape(8, 32, 256)

    v1s, v2s = pl.ds(1024, 256), pl.ds(1280, 256)
    gram = dot3((rh[v1s, :], rl[v1s, :]), (rh[v2s, :], rl[v2s, :]), NT)
    at[:, pl.ds(32, 8), first] = gram[:128].reshape(16, 8, 256)
    at[:, pl.ds(32, 8), second] = gram[128:].reshape(16, 8, 256)

    core_sum = go(remote(("ac",), at.at[pl.ds((1 - c) * 8, 8)], ac, other))
    z_panel(0)
    core_sum.wait_recv()
    for k in range(8):
        at[c * 8 + k] = at[c * 8 + k] + ac[k]
    a0, b0 = c * 8, c * 8 + 4
    one = [go(remote(("ax", d), at.at[a0 + wrap(x + d)], ax.at[d - 1], xid(d))) for d in ODD_FIRST]
    one += [go(remote(("by", d), at.at[b0 + wrap(y + d)], by_.at[d - 1], yid(d))) for d in ODD_FIRST]
    y_panel(2)
    z_panel(1)
    for q in one:
        q.wait_recv()
    as_[0] = (at[a0 + x] + ax[0]) + (ax[1] + ax[2])
    as_[1] = (at[b0 + y] + by_[0]) + (by_[1] + by_[2])
    two = [go(remote(("ay", d), as_.at[0], ay.at[d - 1], yid(d))) for d in ODD_FIRST]
    two += [go(remote(("bx", d), as_.at[1], bx_.at[d - 1], xid(d))) for d in ODD_FIRST]
    y_panel(3)

    def product(h, lo, hi):
        @pl.loop(lo, hi)
        def _(t):
            rows = lanes(t, 256)
            ct[h, :, rows] = dot3((ph[h], plo[h]), (rh[rows, :], rl[rows, :]), NT)

    def early(h):
        arrived(part(z_p_in, h=h), *([part(z_p0_in, k=0)] if h == 0 else [part(z_p0_in, k=1)] if h == 3 else []))

        @pl.loop(0, 4)
        def _(e):
            rows = pl.ds(pl.multiple_of(e * 64, 64), 64)
            ph[h, rows, :], plo[h, rows, :] = split(pk[h, e].reshape(64, W))

        product(h, 4, 6)
        go(remote(("cb", h), ct.at[h, :, pl.ds(pl.multiple_of(1024 + (1 - c) * 256, 256), 256)], cb.at[h], other))
        product(h, 0, 2)
        copy = remote(("cc", h), ct.at[h, :, pl.ds(0, 512)], cc.at[h], other)

        @pl.when(jnp.logical_not(home))
        def _():
            copy.start()

        away_sends.append(copy)

    def along_x(name, h, src, dst):
        out = []
        for f in ODD_FIRST:
            e = wrap(x + f - y + 4)
            out.append(remote((name, f, h), src.at[h, pl.ds(pl.multiple_of(e * 64, 64), 64)], dst.at[h, f - 1], xid(f)))
        return out

    def early_x(h):
        remote(("cb", h), cb.at[h], cb.at[h], other).wait_recv()
        kb[h] = ct[h, :, pl.ds(pl.multiple_of(1024 + c * 256, 256), 256)] + cb[h]
        for q in along_x("xb", h, kb, bx):
            go(q)
        copies = along_x("xc", h, kc, cx)

        @pl.when(home)
        def _():
            remote(("cc", h), cc.at[h], cc.at[h], other).wait_recv()
            kc[h] = ct[h, :, pl.ds(0, 512)] + cc[h]
            for q in copies:
                q.start()

        home_sends.extend(copies)

    def late(h):
        product(h, 2, 4)
        copy = remote(("cc", h), ct.at[h, :, pl.ds(512, 512)], cc.at[h], other)

        @pl.when(home)
        def _():
            copy.start()

        home_sends.append(copy)

    def late_x(h):
        copies = along_x("xc", h, kc, cx)

        @pl.when(jnp.logical_not(home))
        def _():
            remote(("cc", h), cc.at[h], cc.at[h], other).wait_recv()
            kc[h] = ct[h, :, pl.ds(512, 512)] + cc[h]
            for q in copies:
                q.start()

        away_sends.extend(copies)

    mine = pl.ds(pl.multiple_of(wrap(x - y + 4) * 64, 64), 64)

    def finish_b(h):
        for f in ODD_FIRST:
            remote(("xb", f, h), bx.at[h, f - 1], bx.at[h, f - 1], xid(f)).wait_recv()
        sb[h] = (kb[h, mine, :] + bx[h, 0]) + (bx[h, 1] + bx[h, 2])
        here = fb.at[h, :, lanes(c, 256)]
        far = remote(("sb2", h), sb.at[h], here, m_mate)
        near, cross = remote(("sb0", h), sb.at[h], here, other), remote(("sb1", h), sb.at[h], here, swap_mate)

        @pl.when(home)
        def _():
            far.start()
            fb[h, :, lanes(c, 256)] = sb[h]

        @pl.when(jnp.logical_not(home))
        def _():
            cross.start()
            near.start()

        home_sends.append(far)
        away_sends.extend([near, cross])

    def finish_c(h):
        for f in ODD_FIRST:
            remote(("xc", f, h), cx.at[h, f - 1], cx.at[h, f - 1], xid(f)).wait_recv()
        total = (kc[h, mine, :] + cx[h, 0]) + (cx[h, 1] + cx[h, 2])
        copy = remote(("sc", h), sc.at[h], fc.at[h], swap_mate)

        @pl.when(home)
        def _():
            fc[h] = total

        @pl.when(jnp.logical_not(home))
        def _():
            sc[h] = total
            copy.start()

        away_sends.append(copy)

    def final(h):
        @pl.when(home)
        def _():
            ref = fb.at[h, :, lanes(1 - c, 256)]
            remote(("sb0", h), ref, ref, other).wait_recv()

        @pl.when(jnp.logical_not(home))
        def _():
            remote(("sc", h), fc.at[h], fc.at[h], swap_mate).wait_recv()
            ref = fb.at[h, :, lanes(1 - c, 256)]
            remote(("sb1", h), ref, ref, swap_mate).wait_recv()
            ref = fb.at[h, :, lanes(c, 256)]
            remote(("sb2", h), ref, ref, m_mate).wait_recv()

        pair = split(fb[h])
        for cols in (first, second):
            dt[h, :, cols] = fc[h, :, cols] - dot3(pair, (wh[cols, :], wl[cols, :]), NT)
        for d in ODD_FIRST:
            go(remote(("cy", d, h), dt.at[h, :, lanes(wrap(y + d), 128)], cy.at[h, d - 1], yid(d)))

    def done(h):
        for d in ODD_FIRST:
            remote(("cy", d, h), cy.at[h, d - 1], cy.at[h, d - 1], yid(d)).wait_recv()
        res = ((dt[h, :, lanes(y, 128)] + cy[h, 0]) + (cy[h, 1] + cy[h, 2])) / N
        of[pl.ds(h * 32, 32), :] = res[:32]
        of[pl.ds(128 + h * 32, 32), :] = res[32:]

    early(0)
    z_panel(2)
    for q in two:
        q.wait_recv()
    af[a0 + x] = (as_[0] + ay[0]) + (ay[1] + ay[2])
    af[b0 + y] = (as_[1] + bx_[0]) + (bx_[1] + bx_[2])
    for d in ODD_FIRST:
        go(remote(("cx", d), af.at[a0 + x], af.at[a0 + x], xid(d)))
        go(remote(("dy", d), af.at[b0 + y], af.at[b0 + y], yid(d)))
    early_x(0)
    early(1)
    z_panel(3)
    for d in ODD_FIRST:
        ref = af.at[a0 + wrap(x + 4 - d)]
        remote(("cx", d), ref, ref, xid(d)).wait_recv()
        ref = af.at[b0 + wrap(y + 4 - d)]
        remote(("dy", d), ref, ref, yid(d)).wait_recv()
    ref = af.at[pl.ds(c * 8, 8)]
    go(remote(("bc",), ref, ref, other))
    early_x(1)
    ref = af.at[pl.ds((1 - c) * 8, 8)]
    remote(("bc",), ref, ref, other).wait_recv()

    gram = jnp.concatenate([af[:, pl.ds(32, 8), first].reshape(128, 256),
                            af[:, pl.ds(32, 8), second].reshape(128, 256)], axis=0)
    gram2, f1s, f2s = split(gram), split(f1[...]), split(f2[...])
    for t in (0, 1):
        rows = pl.ds(t * 256, 256)
        a1 = af[pl.ds(t * 8, 8), pl.ds(0, 32), first].reshape(256, 256)
        a2 = af[pl.ds(t * 8, 8), pl.ds(0, 32), second].reshape(256, 256)
        w2 = split(dot3(split(a2), f2s, NT))
        wh[rows, second], wl[rows, second] = w2
        w1 = split(dot3(split(a1 - dot3(w2, gram2, NT)), f1s, NT))
        wh[rows, first], wl[rows, first] = w1

    vall = pl.ds(1024, 512)

    @pl.loop(0, 4)
    def _(j):
        cols = pl.ds(pl.multiple_of(j * 256, 256), 256)
        for t in (0, 1):
            rows = pl.ds(t * 256, 256)
            mv[rows, cols] = mk[rows, cols] - dot3((wh[rows, :], wl[rows, :]), (rh[vall, cols], rl[vall, cols]), NN)

    start(*[part(y_r, d=d, half=0) for d in ODD_FIRST])

    def own_r(n):
        return pltpu.make_async_copy(mv.at[mrow(y), pl.ds(0, n * 128)], out_m.at[:, quarter(y, n)], ls.at[4])

    both(lambda n: own_r(n).start())

    early(2)
    arrived(part(z_m0_in, k=0), part(z_m0_in, k=1))
    for e in (1, 3, 2):
        rows = mrow(wrap(y + e))
        both(lambda n: remote(("zm", e), mp.at[rows, pl.ds(0, n * 128)], mp.at[rows, pl.ds(0, n * 128)],
                              m_mate).wait_recv())

    @pl.loop(0, 8)
    def _(i):
        rows = pl.ds(pl.multiple_of(i * 64, 64), 64)
        to = pl.ds(pl.multiple_of(512 + i * 64, 64), 64)
        rh[to, :], rl[to, :] = split(mp[rows, :])

    late(0)
    early_x(2)
    late(1)
    late_x(0)
    late(2)
    late_x(1)
    finish_b(0)
    finish_b(1)
    late_x(2)
    early(3)
    late(3)
    start(*[part(y_r, d=d, half=1) for d in ODD_FIRST])
    early_x(3)
    late_x(3)
    finish_c(0)
    finish_c(1)
    finish_b(2)
    final(0)
    finish_c(2)
    final(1)
    finish_b(3)
    finish_c(3)
    final(2)
    final(3)
    for h in range(4):
        done(h)
    out_c[...] = of[...].T

    arrived(*[part(y_r_in, d=d, half=half) for half in (0, 1) for d in ODD_FIRST])
    both(lambda n: own_r(n).wait())
    both(lambda n: [f(n).wait_send() for f in sends] and None)
    for copy in fixed:
        copy.wait_send()

    @pl.when(home)
    def _():
        for copy in home_sends:
            copy.wait_send()

    @pl.when(jnp.logical_not(home))
    def _():
        for copy in away_sends:
            copy.wait_send()

    assert len(names.ids) <= SEMS, len(names.ids)


SEMS = 160


def shards(modes, prev_modes, first_vectors, first_factor, second_vectors, second_factor):
    any_, vmem = pl.BlockSpec(memory_space=pl.ANY), pl.BlockSpec(memory_space=pltpu.VMEM)
    V = pltpu.VMEM
    dma = pltpu.SemaphoreType.DMA
    return pl.pallas_call(
        kernel,
        out_shape=(jax.ShapeDtypeStruct((128, 3840), F32), jax.ShapeDtypeStruct((128, 256), F32)),
        in_specs=[any_, any_, any_, any_, vmem, vmem],
        out_specs=(any_, vmem),
        scratch_shapes=[
            V((512, W), F32), V((512, W), F32), V((512, W), F32), V((4, 4, 2, 32, W), F32), V((2, 4, 4, 16, W), F32),
            V((1536, W), BF16), V((1536, W), BF16), V((4, 256, W), BF16), V((4, 256, W), BF16),
            V((16, 40, 512), F32), V((8, 40, 512), F32), V((3, 40, 512), F32), V((3, 40, 512), F32),
            V((3, 40, 512), F32), V((3, 40, 512), F32), V((2, 40, 512), F32), V((16, 40, 512), F32),
            V((512, 512), BF16), V((512, 512), BF16),
            V((4, 256, 1536), F32), V((4, 256, 512), F32), V((4, 256, 256), F32),
            V((4, 256, 512), F32), V((4, 256, 256), F32), V((4, 3, 64, 512), F32), V((4, 3, 64, 256), F32),
            V((4, 64, 512), F32), V((4, 64, 256), F32), V((4, 64, 512), F32), V((4, 64, 512), F32),
            V((4, 64, 512), F32), V((4, 3, 64, 128), F32), V((256, 128), F32),
            dma((SEMS,)), dma((SEMS,)), dma((5,)),
        ],
        compiler_params=pltpu.CompilerParams(
            collective_id=0, has_side_effects=True, vmem_limit_bytes=60 * 2**20),
        name="reflect_and_correlate",
    )(modes, prev_modes.reshape(4, 32, 3840), first_vectors, second_vectors, first_factor, second_factor)


def solution(mesh):
    in_specs = (P("col", "row"), P("col", "row"), P("col", "row"), P(), P("col", "row"), P())
    out_specs = (P("col", "row"), P("col", "row"))
    return jax.shard_map(shards, mesh=mesh, in_specs=in_specs, out_specs=out_specs, check_vma=False)
```

```python
import functools

import jax
import jax.numpy as jnp
from jax import lax
from jax.experimental import pallas as pl
from jax.experimental.pallas import tpu as pltpu
from jax.sharding import PartitionSpec as P

N = 30720
MESH = pl.DeviceIdType.MESH
F32 = jnp.float32
BF16 = jnp.bfloat16
W = 1024
ODD_FIRST = (1, 3, 2)


def split(value):
    high = value.astype(BF16)
    return high, (value - high.astype(F32)).astype(BF16)


def dot3(left, right, dims):
    (lh, ll), (rh, rl) = left, right
    mul = functools.partial(lax.dot_general, dimension_numbers=(dims, ((), ())), preferred_element_type=F32)
    return mul(lh, rh) + (mul(lh, rl) + mul(ll, rh))


NT = ((1,), (1,))
NN = ((1,), (0,))


class Names:
    def __init__(self):
        self.ids = {}

    def __call__(self, *name):
        return self.ids.setdefault(name, len(self.ids))


def kernel(m_in, p_in, v1_in, v2_in, f1, f2, out_m, out_c,
           mk, mp, mv, pk, vk, rh, rl, ph, plo, at, ac, ax, ay, bx_, by_, as_, af, wh, wl,
           ct, bt, cc, cb, kc, kb, cx, bx, sc, sb, fc, fb, dt, cy, of, ss, rs, ls):
    r, col = lax.axis_index("row"), lax.axis_index("col")
    x, c = lax.div(r, 2), lax.rem(r, 2)
    y, z = lax.div(col, 4), lax.rem(col, 4)
    eight = lax.rem(y + c, 2) == 0
    home = c == lax.div(z, 2)
    zl = lax.rem(z, 2)

    def wrap(a):
        return lax.rem(a, 4)

    def yid(d):
        return (r, wrap(y + d) * 4 + z)

    def zid(d):
        return (r, y * 4 + wrap(z + d))

    def xid(d):
        return (wrap(x + d) * 2 + c, col)

    other = (x * 2 + 1 - c, col)
    p_mate = (r, y * 4 + z + 1 - 2 * zl)
    m_mate = (r, y * 4 + 3 - z)
    swap_mate = (x * 2 + 1 - c, y * 4 + 3 - z)
    names = Names()

    def both(fn):
        @pl.when(eight)
        def _():
            fn(8)

        @pl.when(jnp.logical_not(eight))
        def _():
            fn(7)

    def remote(name, src, dst, dev):
        i = names(*name)
        return pltpu.make_async_remote_copy(
            src_ref=src, dst_ref=dst, send_sem=ss.at[i], recv_sem=rs.at[i], device_id=dev, device_id_type=MESH)

    def quarter(q, n):
        start = 15 * lax.div(q, 2) + lax.rem(q, 2) * (8 - c)
        return pl.ds(pl.multiple_of(start * 128, 128), n * 128)

    def width(n, d):
        return 15 - n if d % 2 else n

    def mrow(yy, first=0, count=128):
        return pl.ds(pl.multiple_of(yy * 128 + first, 32), count)

    def lanes(i, step):
        return pl.ds(pl.multiple_of(i * step, step), step)

    sends = []
    fixed = []
    home_sends, away_sends = [], []

    def y_v(n, d, p):
        nd, q = width(n, d), wrap(y + d)
        src = (v1_in, v2_in)[p]
        return remote(("yv", d, p), src.at[:, quarter(q, nd)], vk.at[p, y, z, :, pl.ds(0, nd * 128)], yid(d))

    def y_v_in(n, d, p):
        dst = vk.at[p, wrap(y + 4 - d), z, :, pl.ds(0, n * 128)]
        return remote(("yv", d, p), dst, dst, yid(d))

    def y_m(n, d):
        nd, q = width(n, d), wrap(y + d)
        return remote(("ym", d), m_in.at[:, quarter(q, nd)], mk.at[mrow(y), pl.ds(0, nd * 128)], yid(d))

    def y_m_in(n, d):
        dst = mk.at[mrow(wrap(y + 4 - d)), pl.ds(0, n * 128)]
        return remote(("ym", d), dst, dst, yid(d))

    def y_p(n, d, h):
        nd, q = width(n, d), wrap(y + d)
        return remote(("yp", d, h), p_in.at[h, :, quarter(q, nd)], pk.at[h, 4 - d, zl, :, pl.ds(0, nd * 128)], yid(d))

    def y_p_in(n, d, h):
        dst = pk.at[h, 4 - d, zl, :, pl.ds(0, n * 128)]
        return remote(("yp", d, h), dst, dst, yid(d))

    def z_v(n, s, p):
        ref = vk.at[p, :, z, :, pl.ds(0, n * 128)]
        return remote(("zv", s, p), ref, ref, zid(s))

    def z_v_in(n, s, p):
        ref = vk.at[p, :, wrap(z + 4 - s), :, pl.ds(0, n * 128)]
        return remote(("zv", s, p), ref, ref, zid(s))

    def z_vf(n, s):
        ref = vk.at[0 if s == 1 else 1, :, wrap(z + 4 - s), :, pl.ds(0, n * 128)]
        return remote(("zvf", s), ref, ref, zid(s))

    def z_vf_in(n, s):
        ref = vk.at[0 if s == 1 else 1, :, wrap(z + 2), :, pl.ds(0, n * 128)]
        return remote(("zvf", s), ref, ref, zid(s))

    def z_m0(n, k):
        a, b = ((0, 96), (96, 32))[k]
        return remote(("zm0", k), m_in.at[pl.ds(a, b), quarter(y, n)], mp.at[mrow(y, a, b), pl.ds(0, n * 128)], m_mate)

    def z_m0_in(n, k):
        a, b = ((0, 96), (96, 32))[k]
        ref = mp.at[mrow(y, a, b), pl.ds(0, n * 128)]
        return remote(("zm0", k), ref, ref, m_mate)

    def z_m(n, e):
        rows = mrow(wrap(y + e))
        return remote(("zm", e), mk.at[rows, pl.ds(0, n * 128)], mp.at[rows, pl.ds(0, n * 128)], m_mate)

    def z_p0(n, k):
        a, b = ((0, 3), (3, 1))[k]
        return remote(("zp0", k), p_in.at[pl.ds(a, b), :, quarter(y, n)],
                      pk.at[pl.ds(a, b), 0, zl, :, pl.ds(0, n * 128)], p_mate)

    def z_p0_in(n, k):
        a, b = ((0, 3), (3, 1))[k]
        ref = pk.at[pl.ds(a, b), 0, 1 - zl, :, pl.ds(0, n * 128)]
        return remote(("zp0", k), ref, ref, p_mate)

    def z_p(n, h):
        ref = pk.at[h, pl.ds(1, 3), zl, :, pl.ds(0, n * 128)]
        return remote(("zp", h), ref, ref, p_mate)

    def z_pe(n, e, h):
        ref = pk.at[h, e, zl, :, pl.ds(0, n * 128)]
        return remote(("zpe", e, h), ref, ref, p_mate)

    def z_pe_in(n, e, h):
        ref = pk.at[h, e, 1 - zl, :, pl.ds(0, n * 128)]
        return remote(("zpe", e, h), ref, ref, p_mate)

    def z_p_in(n, h):
        ref = pk.at[h, pl.ds(1, 3), 1 - zl, :, pl.ds(0, n * 128)]
        return remote(("zp", h), ref, ref, p_mate)

    def y_r(n, d, half):
        return remote(("yr", d, half), mv.at[mrow(wrap(y + d), half * 64, 64), pl.ds(0, n * 128)],
                      out_m.at[pl.ds(half * 64, 64), quarter(y, n)], yid(d))

    def y_r_in(n, d, half):
        dst = out_m.at[pl.ds(half * 64, 64), quarter(wrap(y + 4 - d), width(n, d))]
        return remote(("yr", d, half), dst, dst, yid(d))

    def start(*fns):
        both(lambda n: [f(n).start() for f in fns] and None)
        sends.extend(fns)

    def arrived(*fns):
        both(lambda n: [f(n).wait_recv() for f in fns] and None)

    def go(copy):
        copy.start()
        fixed.append(copy)
        return copy

    part = functools.partial

    def drain():
        widths, plain, here, there = list(sends), list(fixed), list(home_sends), list(away_sends)
        both(lambda n: [f(n).wait_send() for f in widths] and None)
        for copy in plain:
            copy.wait_send()

        @pl.when(home)
        def _():
            for copy in here:
                copy.wait_send()

        @pl.when(jnp.logical_not(home))
        def _():
            for copy in there:
                copy.wait_send()

        for held in (sends, fixed, home_sends, away_sends):
            held.clear()

    @pl.when(jnp.logical_not(eight))
    def _():
        pad = pl.ds(896, 128)
        mk[:, pad] = jnp.zeros((512, 128), F32)
        mp[:, pad] = jnp.zeros((512, 128), F32)
        pk[:, :, :, :, pad] = jnp.zeros((4, 4, 2, 32, 128), F32)
        vk[:, :, :, :, pad] = jnp.zeros((2, 4, 4, 16, 128), F32)

    barrier = pltpu.get_barrier_semaphore()
    peers = [yid(1), yid(2), yid(3), xid(1), xid(2), xid(3), other, zid(1), zid(2), zid(3)]
    peers += [(x * 2 + 1 - c, y * 4 + wrap(z + d)) for d in (1, 2, 3)]
    for dev in peers:
        pl.semaphore_signal(barrier, inc=1, device_id=dev, device_id_type=MESH)
    pl.semaphore_wait(barrier, len(peers))

    start(*[part(y_v, d=d, p=p) for d in ODD_FIRST for p in (0, 1)])
    start(part(z_p0, k=0), part(z_m0, k=0))

    def own(n):
        return [
            pltpu.make_async_copy(v1_in.at[:, quarter(y, n)], vk.at[0, y, z, :, pl.ds(0, n * 128)], ls.at[0]),
            pltpu.make_async_copy(v2_in.at[:, quarter(y, n)], vk.at[1, y, z, :, pl.ds(0, n * 128)], ls.at[1]),
            pltpu.make_async_copy(m_in.at[:, quarter(y, n)], mk.at[mrow(y), pl.ds(0, n * 128)], ls.at[2]),
            pltpu.make_async_copy(p_in.at[:, :, quarter(y, n)], pk.at[:, 0, zl, :, pl.ds(0, n * 128)], ls.at[3]),
        ]

    both(lambda n: [q.start() for q in own(n)] and None)
    start(*[part(y_m, d=d) for d in ODD_FIRST])

    def y_panel(h):
        start(*[part(y_p, d=d, h=h) for d in ODD_FIRST])

    def z_panel(h):
        arrived(*[part(y_p_in, d=d, h=h) for d in ODD_FIRST])
        start(part(z_p, h=h))

    y_panel(0)
    y_panel(1)

    arrived(*[part(y_v_in, d=d, p=p) for d in ODD_FIRST for p in (0, 1)])
    both(lambda n: [q.wait() for q in own(n)] and None)
    start(part(z_v, s=1, p=0), part(z_v, s=3, p=1), part(z_v, s=1, p=1), part(z_v, s=3, p=0))
    arrived(part(z_v_in, s=1, p=0))
    start(part(z_vf, s=1))
    arrived(part(z_v_in, s=3, p=1))
    start(part(z_vf, s=3))
    start(part(z_p0, k=1), part(z_m0, k=1))
    for e in (1, 3, 2):
        arrived(part(y_m_in, d=4 - e))
        start(part(z_m, e=e))

    @pl.loop(0, 8)
    def _(i):
        rows = pl.ds(pl.multiple_of(i * 64, 64), 64)
        rh[rows, :], rl[rows, :] = split(mk[rows, :])

    arrived(part(z_v_in, s=1, p=1), part(z_v_in, s=3, p=0), part(z_vf_in, s=1), part(z_vf_in, s=3))

    @pl.loop(0, 8)
    def _(i):
        p, yy = lax.div(i, 4), lax.rem(i, 4)
        rows = pl.ds(pl.multiple_of(1024 + i * 64, 64), 64)
        rh[rows, :], rl[rows, :] = split(vk[p, yy].reshape(64, W))

    first, second = pl.ds(0, 256), pl.ds(256, 256)

    for t in (0, 1):
        rows = pl.ds(t * 256, 256)
        for j, cols in ((0, first), (1, second)):
            vrows = pl.ds(1024 + j * 256, 256)
            res = dot3((rh[rows, :], rl[rows, :]), (rh[vrows, :], rl[vrows, :]), NT)
            at[pl.ds(t * 8, 8), pl.ds(0, 32), cols] = res.reshape(8, 32, 256)

    v1s, v2s = pl.ds(1024, 256), pl.ds(1280, 256)
    gram = dot3((rh[v1s, :], rl[v1s, :]), (rh[v2s, :], rl[v2s, :]), NT)
    at[:, pl.ds(32, 8), first] = gram[:128].reshape(16, 8, 256)
    at[:, pl.ds(32, 8), second] = gram[128:].reshape(16, 8, 256)

    core_sum = go(remote(("ac",), at.at[pl.ds((1 - c) * 8, 8)], ac, other))
    z_panel(0)
    core_sum.wait_recv()
    for k in range(8):
        at[c * 8 + k] = at[c * 8 + k] + ac[k]
    a0, b0 = c * 8, c * 8 + 4
    one = [go(remote(("ax", d), at.at[a0 + wrap(x + d)], ax.at[d - 1], xid(d))) for d in ODD_FIRST]
    one += [go(remote(("by", d), at.at[b0 + wrap(y + d)], by_.at[d - 1], yid(d))) for d in ODD_FIRST]
    y_panel(2)
    z_panel(1)
    for q in one:
        q.wait_recv()
    as_[0] = (at[a0 + x] + ax[0]) + (ax[1] + ax[2])
    as_[1] = (at[b0 + y] + by_[0]) + (by_[1] + by_[2])
    two = [go(remote(("ay", d), as_.at[0], ay.at[d - 1], yid(d))) for d in ODD_FIRST]
    two += [go(remote(("bx", d), as_.at[1], bx_.at[d - 1], xid(d))) for d in ODD_FIRST]

    def product(h, lo, hi):
        for t in range(lo, hi):
            rows = pl.ds(t * 256, 256)
            ct[h, :, rows] = dot3((ph[h], plo[h]), (rh[rows, :], rl[rows, :]), NT)

    def landed(h):
        arrived(*([part(z_pe_in, e=e, h=h) for e in (1, 3, 2)] if h == 3 else [part(z_p_in, h=h)]),
                *([part(z_p0_in, k=0)] if h == 0 else [part(z_p0_in, k=1)] if h == 3 else []))

        @pl.loop(0, 4)
        def _(e):
            rows = pl.ds(pl.multiple_of(e * 64, 64), 64)
            ph[h, rows, :], plo[h, rows, :] = split(pk[h, e].reshape(64, W))

    def early(h):
        panel = pl.ds(pl.multiple_of(1024 + zl * 256, 256), 256)
        bt[h] = dot3((ph[h], plo[h]), (rh[panel, :], rl[panel, :]), NT)
        go(remote(("cb", h), bt.at[h, :, lanes(1 - c, 128)], cb.at[h], other))
        product(h, 0, 2)
        copy = remote(("cc", h), ct.at[h, :, pl.ds(0, 512)], cc.at[h], other)

        @pl.when(jnp.logical_not(home))
        def _():
            copy.start()

        away_sends.append(copy)

    def along_x(name, h, src, dst):
        out = []
        for f in ODD_FIRST:
            e = wrap(x + f - y + 4)
            out.append(remote((name, f, h), src.at[h, pl.ds(pl.multiple_of(e * 64, 64), 64)], dst.at[h, f - 1], xid(f)))
        return out

    def early_x(h):
        remote(("cb", h), cb.at[h], cb.at[h], other).wait_recv()
        kb[h] = bt[h, :, lanes(c, 128)] + cb[h]
        for q in along_x("xb", h, kb, bx):
            go(q)
        copies = along_x("xc", h, kc, cx)

        @pl.when(home)
        def _():
            remote(("cc", h), cc.at[h], cc.at[h], other).wait_recv()
            kc[h] = ct[h, :, pl.ds(0, 512)] + cc[h]
            for q in copies:
                q.start()

        home_sends.extend(copies)

    def late(h):
        product(h, 2, 4)
        copy = remote(("cc", h), ct.at[h, :, pl.ds(512, 512)], cc.at[h], other)

        @pl.when(home)
        def _():
            copy.start()

        home_sends.append(copy)

    def late_x(h):
        copies = along_x("xc", h, kc, cx)

        @pl.when(jnp.logical_not(home))
        def _():
            remote(("cc", h), cc.at[h], cc.at[h], other).wait_recv()
            kc[h] = ct[h, :, pl.ds(512, 512)] + cc[h]
            for q in copies:
                q.start()

        away_sends.extend(copies)

    mine = pl.ds(pl.multiple_of(wrap(x - y + 4) * 64, 64), 64)

    pair = lax.div(z, 2)
    b_slot = zl * 2 + c

    def b_copies(h):
        base = names("sbr", h, 0)
        for k in (1, 2, 3):
            names("sbr", h, k)
        return [pltpu.make_async_remote_copy(
            src_ref=sb.at[h], dst_ref=fb.at[h, :, lanes(b_slot, 128)], send_sem=ss.at[names("sbs", h, k)],
            recv_sem=rs.at[base + b_slot], device_id=(x * 2 + pair, y * 4 + wrap(z + k)), device_id_type=MESH)
            for k in range(4)]

    def finish_b(h):
        for f in ODD_FIRST:
            remote(("xb", f, h), bx.at[h, f - 1], bx.at[h, f - 1], xid(f)).wait_recv()
        sb[h] = (kb[h, mine, :] + bx[h, 0]) + (bx[h, 1] + bx[h, 2])
        copies = b_copies(h)
        for q in copies[1:]:
            go(q)

        @pl.when(home)
        def _():
            fb[h, :, lanes(b_slot, 128)] = sb[h]

        @pl.when(jnp.logical_not(home))
        def _():
            copies[0].start()

        away_sends.append(copies[0])

    def finish_c(h):
        for f in ODD_FIRST:
            remote(("xc", f, h), cx.at[h, f - 1], cx.at[h, f - 1], xid(f)).wait_recv()
        total = (kc[h, mine, :] + cx[h, 0]) + (cx[h, 1] + cx[h, 2])
        copy = remote(("sc", h), sc.at[h], fc.at[h], swap_mate)

        @pl.when(home)
        def _():
            fc[h] = total

        @pl.when(jnp.logical_not(home))
        def _():
            sc[h] = total
            copy.start()

        away_sends.append(copy)

    def final(h):
        for k in range(4):
            @pl.when(jnp.logical_not(jnp.logical_and(home, b_slot == k)))
            def _():
                ref = fb.at[h, :, pl.ds(k * 128, 128)]
                remote(("sbr", h, k), ref, ref, other).wait_recv()

        @pl.when(jnp.logical_not(home))
        def _():
            remote(("sc", h), fc.at[h], fc.at[h], swap_mate).wait_recv()

        fbs = split(fb[h])
        for cols in (first, second):
            dt[h, :, cols] = fc[h, :, cols] - dot3(fbs, (wh[cols, :], wl[cols, :]), NT)
        for d in ODD_FIRST:
            go(remote(("cy", d, h), dt.at[h, :, lanes(wrap(y + d), 128)], cy.at[h, d - 1], yid(d)))

    def done(h):
        for d in ODD_FIRST:
            remote(("cy", d, h), cy.at[h, d - 1], cy.at[h, d - 1], yid(d)).wait_recv()
        res = ((dt[h, :, lanes(y, 128)] + cy[h, 0]) + (cy[h, 1] + cy[h, 2])) / N
        of[pl.ds(h * 32, 32), :] = res[:32]
        of[pl.ds(128 + h * 32, 32), :] = res[32:]

    landed(0)
    early(0)
    early_x(0)
    z_panel(2)
    for q in two:
        q.wait_recv()
    af[a0 + x] = (as_[0] + ay[0]) + (ay[1] + ay[2])
    af[b0 + y] = (as_[1] + bx_[0]) + (bx_[1] + bx_[2])
    for d in ODD_FIRST:
        go(remote(("cx", d), af.at[a0 + x], af.at[a0 + x], xid(d)))
        go(remote(("dy", d), af.at[b0 + y], af.at[b0 + y], yid(d)))
    y_panel(3)
    landed(1)
    early(1)
    early_x(1)
    for d in ODD_FIRST:
        ref = af.at[a0 + wrap(x + 4 - d)]
        remote(("cx", d), ref, ref, xid(d)).wait_recv()
        ref = af.at[b0 + wrap(y + 4 - d)]
        remote(("dy", d), ref, ref, yid(d)).wait_recv()
    ref = af.at[pl.ds(c * 8, 8)]
    go(remote(("bc",), ref, ref, other))
    landed(2)
    early(2)
    ref = af.at[pl.ds((1 - c) * 8, 8)]
    remote(("bc",), ref, ref, other).wait_recv()


    early_x(2)

    def z_last(*es):
        arrived(*[part(y_p_in, d=4 - e, h=3) for e in es])
        start(*[part(z_pe, e=e, h=3) for e in es])

    z_last(1, 3)

    gram = jnp.concatenate([af[:, pl.ds(32, 8), first].reshape(128, 256),
                            af[:, pl.ds(32, 8), second].reshape(128, 256)], axis=0)
    gram2, f1s, f2s = split(gram), split(f1[...]), split(f2[...])
    for t in (0, 1):
        rows = pl.ds(t * 256, 256)
        a1 = af[pl.ds(t * 8, 8), pl.ds(0, 32), first].reshape(256, 256)
        a2 = af[pl.ds(t * 8, 8), pl.ds(0, 32), second].reshape(256, 256)
        w2 = split(dot3(split(a2), f2s, NT))
        wh[rows, second], wl[rows, second] = w2
        w1 = split(dot3(split(a1 - dot3(w2, gram2, NT)), f1s, NT))
        wh[rows, first], wl[rows, first] = w1

    vall = pl.ds(1024, 512)

    def move(d):
        rows = mrow(wrap(y + d))
        for k in range(2):
            cols = pl.ds(k * 512, 512)
            mv[rows, cols] = mk[rows, cols] - dot3((wh[rows, :], wl[rows, :]), (rh[vall, cols], rl[vall, cols]), NN)

    def own_r(n):
        return pltpu.make_async_copy(mv.at[mrow(y), pl.ds(0, n * 128)], out_m.at[:, quarter(y, n)], ls.at[4])

    def modes_landed():
        arrived(part(z_m0_in, k=0), part(z_m0_in, k=1))
        for e in (1, 3, 2):
            rows = mrow(wrap(y + e))
            both(lambda n: remote(("zm", e), mp.at[rows, pl.ds(0, n * 128)], mp.at[rows, pl.ds(0, n * 128)],
                                  m_mate).wait_recv())

        @pl.loop(0, 8)
        def _(i):
            rows = pl.ds(pl.multiple_of(i * 64, 64), 64)
            to = pl.ds(pl.multiple_of(512 + i * 64, 64), 64)
            rh[to, :], rl[to, :] = split(mp[rows, :])

    move(1)
    start(part(y_r, d=1, half=0))
    move(3)
    start(part(y_r, d=3, half=0))
    z_last(2)
    modes_landed()
    late(0)
    move(2)
    start(part(y_r, d=2, half=0))
    late_x(0)
    move(0)
    both(lambda n: own_r(n).start())
    late(1)
    late(2)
    late_x(1)
    late_x(2)
    start(*[part(y_r, d=d, half=1) for d in ODD_FIRST])
    finish_b(0)
    finish_b(1)
    landed(3)
    late(3)
    early(3)
    late_x(3)
    early_x(3)
    finish_c(0)
    finish_c(1)
    finish_b(2)
    final(0)
    finish_c(2)
    final(1)
    finish_b(3)
    finish_c(3)
    final(2)
    done(0)
    done(1)
    final(3)
    drain()
    done(2)
    done(3)
    out_c[...] = of[...].T

    arrived(*[part(y_r_in, d=d, half=half) for half in (0, 1) for d in ODD_FIRST])
    both(lambda n: own_r(n).wait())
    assert len(names.ids) <= SEMS, len(names.ids)


SEMS = 192


def shards(modes, prev_modes, first_vectors, first_factor, second_vectors, second_factor):
    any_, vmem = pl.BlockSpec(memory_space=pl.ANY), pl.BlockSpec(memory_space=pltpu.VMEM)
    V = pltpu.VMEM
    dma = pltpu.SemaphoreType.DMA
    return pl.pallas_call(
        kernel,
        out_shape=(jax.ShapeDtypeStruct((128, 3840), F32), jax.ShapeDtypeStruct((128, 256), F32)),
        in_specs=[any_, any_, any_, any_, vmem, vmem],
        out_specs=(any_, vmem),
        scratch_shapes=[
            V((512, W), F32), V((512, W), F32), V((512, W), F32), V((4, 4, 2, 32, W), F32), V((2, 4, 4, 16, W), F32),
            V((1536, W), BF16), V((1536, W), BF16), V((4, 256, W), BF16), V((4, 256, W), BF16),
            V((16, 40, 512), F32), V((8, 40, 512), F32), V((3, 40, 512), F32), V((3, 40, 512), F32),
            V((3, 40, 512), F32), V((3, 40, 512), F32), V((2, 40, 512), F32), V((16, 40, 512), F32),
            V((512, 512), BF16), V((512, 512), BF16),
            V((4, 256, 1024), F32), V((4, 256, 256), F32), V((4, 256, 512), F32), V((4, 256, 128), F32),
            V((4, 256, 512), F32), V((4, 256, 128), F32), V((4, 3, 64, 512), F32), V((4, 3, 64, 128), F32),
            V((4, 64, 512), F32), V((4, 64, 128), F32), V((4, 64, 512), F32), V((4, 64, 512), F32),
            V((4, 64, 512), F32), V((4, 3, 64, 128), F32), V((256, 128), F32),
            dma((SEMS,)), dma((SEMS,)), dma((5,)),
        ],
        compiler_params=pltpu.CompilerParams(
            collective_id=0, has_side_effects=True, vmem_limit_bytes=60 * 2**20),
        name="reflect_and_correlate",
    )(modes, prev_modes.reshape(4, 32, 3840), first_vectors, second_vectors, first_factor, second_factor)


def solution(mesh):
    in_specs = (P("col", "row"), P("col", "row"), P("col", "row"), P(), P("col", "row"), P())
    out_specs = (P("col", "row"), P("col", "row"))
    return jax.shard_map(shards, mesh=mesh, in_specs=in_specs, out_specs=out_specs, check_vma=False)
```

```python
import functools

import jax
import jax.numpy as jnp
from jax import lax
from jax.experimental import pallas as pl
from jax.experimental.pallas import tpu as pltpu
from jax.sharding import PartitionSpec as P

N = 30720
MESH = pl.DeviceIdType.MESH
F32 = jnp.float32
BF16 = jnp.bfloat16
W = 1024
ODD_FIRST = (1, 3, 2)


def split(value):
    high = value.astype(BF16)
    return high, (value - high.astype(F32)).astype(BF16)


def dot3(left, right, dims):
    (lh, ll), (rh, rl) = left, right
    mul = functools.partial(lax.dot_general, dimension_numbers=(dims, ((), ())), preferred_element_type=F32)
    return mul(lh, rh) + (mul(lh, rl) + mul(ll, rh))


NT = ((1,), (1,))
NN = ((1,), (0,))


class Names:
    def __init__(self):
        self.ids = {}

    def __call__(self, *name):
        return self.ids.setdefault(name, len(self.ids))


def kernel(m_in, p_in, v1_in, v2_in, f1, f2, out_m, out_c,
           mk, mp, mv, pk, vk, rh, rl, ph, plo, at, ac, ax, ay, bx_, by_, as_, af, wh, wl,
           ct, bt, cc, cb, kc, kb, cx, bx, sc, sb, fc, fb, dt, cy, of, ss, rs, ls):
    r, col = lax.axis_index("row"), lax.axis_index("col")
    x, c = lax.div(r, 2), lax.rem(r, 2)
    y, z = lax.div(col, 4), lax.rem(col, 4)
    eight = lax.rem(y + c, 2) == 0
    home = c == lax.div(z, 2)
    zl = lax.rem(z, 2)

    def wrap(a):
        return lax.rem(a, 4)

    def yid(d):
        return (r, wrap(y + d) * 4 + z)

    def zid(d):
        return (r, y * 4 + wrap(z + d))

    def xid(d):
        return (wrap(x + d) * 2 + c, col)

    other = (x * 2 + 1 - c, col)
    p_mate = (r, y * 4 + z + 1 - 2 * zl)
    m_mate = (r, y * 4 + 3 - z)
    swap_mate = (x * 2 + 1 - c, y * 4 + 3 - z)
    names = Names()

    def both(fn):
        @pl.when(eight)
        def _():
            fn(8)

        @pl.when(jnp.logical_not(eight))
        def _():
            fn(7)

    def remote(name, src, dst, dev):
        i = names(*name)
        return pltpu.make_async_remote_copy(
            src_ref=src, dst_ref=dst, send_sem=ss.at[i], recv_sem=rs.at[i], device_id=dev, device_id_type=MESH)

    def quarter(q, n):
        start = 15 * lax.div(q, 2) + lax.rem(q, 2) * (8 - c)
        return pl.ds(pl.multiple_of(start * 128, 128), n * 128)

    def width(n, d):
        return 15 - n if d % 2 else n

    def mrow(yy, first=0, count=128):
        return pl.ds(pl.multiple_of(yy * 128 + first, 32), count)

    def lanes(i, step):
        return pl.ds(pl.multiple_of(i * step, step), step)

    sends = []
    fixed = []
    home_sends, away_sends = [], []

    def y_v(n, d, p):
        nd, q = width(n, d), wrap(y + d)
        src = (v1_in, v2_in)[p]
        return remote(("yv", d, p), src.at[:, quarter(q, nd)], vk.at[p, y, z, :, pl.ds(0, nd * 128)], yid(d))

    def y_v_in(n, d, p):
        dst = vk.at[p, wrap(y + 4 - d), z, :, pl.ds(0, n * 128)]
        return remote(("yv", d, p), dst, dst, yid(d))

    def y_m(n, d):
        nd, q = width(n, d), wrap(y + d)
        return remote(("ym", d), m_in.at[:, quarter(q, nd)], mk.at[mrow(y), pl.ds(0, nd * 128)], yid(d))

    def y_m_in(n, d):
        dst = mk.at[mrow(wrap(y + 4 - d)), pl.ds(0, n * 128)]
        return remote(("ym", d), dst, dst, yid(d))

    def y_p(n, d, h):
        nd, q = width(n, d), wrap(y + d)
        return remote(("yp", d, h), p_in.at[h, :, quarter(q, nd)], pk.at[h, 4 - d, zl, :, pl.ds(0, nd * 128)], yid(d))

    def y_p_in(n, d, h):
        dst = pk.at[h, 4 - d, zl, :, pl.ds(0, n * 128)]
        return remote(("yp", d, h), dst, dst, yid(d))

    def z_v(n, to, p):
        ref = vk.at[p, :, z, :, pl.ds(0, n * 128)]
        return remote(("zv", to, p), ref, ref, p_mate if to == "p" else m_mate)

    def z_v_in(n, to, p):
        ref = vk.at[p, :, (z + 1 - 2 * zl) if to == "p" else 3 - z, :, pl.ds(0, n * 128)]
        return remote(("zv", to, p), ref, ref, p_mate)

    def z_vf(n, p):
        ref = vk.at[p, :, 3 - z, :, pl.ds(0, n * 128)]
        return remote(("zvf", p), ref, ref, p_mate)

    def z_vf_in(n, p):
        ref = vk.at[p, :, wrap(z + 2), :, pl.ds(0, n * 128)]
        return remote(("zvf", p), ref, ref, p_mate)

    def z_m0(n, k):
        a, b = ((0, 96), (96, 32))[k]
        return remote(("zm0", k), m_in.at[pl.ds(a, b), quarter(y, n)], mp.at[mrow(y, a, b), pl.ds(0, n * 128)], m_mate)

    def z_m0_in(n, k):
        a, b = ((0, 96), (96, 32))[k]
        ref = mp.at[mrow(y, a, b), pl.ds(0, n * 128)]
        return remote(("zm0", k), ref, ref, m_mate)

    def z_m(n, e):
        rows = mrow(wrap(y + e))
        return remote(("zm", e), mk.at[rows, pl.ds(0, n * 128)], mp.at[rows, pl.ds(0, n * 128)], m_mate)

    def z_p0(n, k):
        a, b = ((0, 3), (3, 1))[k]
        return remote(("zp0", k), p_in.at[pl.ds(a, b), :, quarter(y, n)],
                      pk.at[pl.ds(a, b), 0, zl, :, pl.ds(0, n * 128)], p_mate)

    def z_p0_in(n, k):
        a, b = ((0, 3), (3, 1))[k]
        ref = pk.at[pl.ds(a, b), 0, 1 - zl, :, pl.ds(0, n * 128)]
        return remote(("zp0", k), ref, ref, p_mate)

    def z_p(n, h):
        ref = pk.at[h, pl.ds(1, 3), zl, :, pl.ds(0, n * 128)]
        return remote(("zp", h), ref, ref, p_mate)

    def z_pe(n, e, h):
        ref = pk.at[h, e, zl, :, pl.ds(0, n * 128)]
        return remote(("zpe", e, h), ref, ref, p_mate)

    def z_pe_in(n, e, h):
        ref = pk.at[h, e, 1 - zl, :, pl.ds(0, n * 128)]
        return remote(("zpe", e, h), ref, ref, p_mate)

    def z_p_in(n, h):
        ref = pk.at[h, pl.ds(1, 3), 1 - zl, :, pl.ds(0, n * 128)]
        return remote(("zp", h), ref, ref, p_mate)

    def y_r(n, d, half):
        return remote(("yr", d, half), mv.at[mrow(wrap(y + d), half * 64, 64), pl.ds(0, n * 128)],
                      out_m.at[pl.ds(half * 64, 64), quarter(y, n)], yid(d))

    def y_r_in(n, d, half):
        dst = out_m.at[pl.ds(half * 64, 64), quarter(wrap(y + 4 - d), width(n, d))]
        return remote(("yr", d, half), dst, dst, yid(d))

    def start(*fns):
        both(lambda n: [f(n).start() for f in fns] and None)
        sends.extend(fns)

    def arrived(*fns):
        both(lambda n: [f(n).wait_recv() for f in fns] and None)

    def go(copy):
        copy.start()
        fixed.append(copy)
        return copy

    part = functools.partial

    def drain():
        widths, plain, here, there = list(sends), list(fixed), list(home_sends), list(away_sends)
        both(lambda n: [f(n).wait_send() for f in widths] and None)
        for copy in plain:
            copy.wait_send()

        @pl.when(home)
        def _():
            for copy in here:
                copy.wait_send()

        @pl.when(jnp.logical_not(home))
        def _():
            for copy in there:
                copy.wait_send()

        for held in (sends, fixed, home_sends, away_sends):
            held.clear()

    @pl.when(jnp.logical_not(eight))
    def _():
        pad = pl.ds(896, 128)
        mk[:, pad] = jnp.zeros((512, 128), F32)
        mp[:, pad] = jnp.zeros((512, 128), F32)
        pk[:, :, :, :, pad] = jnp.zeros((4, 4, 2, 32, 128), F32)
        vk[:, :, :, :, pad] = jnp.zeros((2, 4, 4, 16, 128), F32)

    barrier = pltpu.get_barrier_semaphore()
    peers = [yid(1), yid(2), yid(3), xid(1), xid(2), xid(3), other, zid(1), zid(2), zid(3)]
    peers += [(x * 2 + 1 - c, y * 4 + wrap(z + d)) for d in (1, 2, 3)]
    for dev in peers:
        pl.semaphore_signal(barrier, inc=1, device_id=dev, device_id_type=MESH)
    pl.semaphore_wait(barrier, len(peers))

    start(*[part(y_v, d=d, p=p) for d in ODD_FIRST for p in (0, 1)])
    start(part(z_p0, k=0), part(z_m0, k=0))

    def own(n):
        return [
            pltpu.make_async_copy(v1_in.at[:, quarter(y, n)], vk.at[0, y, z, :, pl.ds(0, n * 128)], ls.at[0]),
            pltpu.make_async_copy(v2_in.at[:, quarter(y, n)], vk.at[1, y, z, :, pl.ds(0, n * 128)], ls.at[1]),
            pltpu.make_async_copy(m_in.at[:, quarter(y, n)], mk.at[mrow(y), pl.ds(0, n * 128)], ls.at[2]),
            pltpu.make_async_copy(p_in.at[:, :, quarter(y, n)], pk.at[:, 0, zl, :, pl.ds(0, n * 128)], ls.at[3]),
        ]

    both(lambda n: [q.start() for q in own(n)] and None)

    def y_panel(h, ds=ODD_FIRST):
        start(*[part(y_p, d=d, h=h) for d in ds])

    def z_panel(h):
        arrived(*[part(y_p_in, d=d, h=h) for d in ODD_FIRST])
        start(part(z_p, h=h))

    start(*[part(y_m, d=d) for d in ODD_FIRST])
    y_panel(0)
    y_panel(1)

    arrived(*[part(y_v_in, d=d, p=p) for d in ODD_FIRST for p in (0, 1)])
    both(lambda n: [q.wait() for q in own(n)] and None)
    start(*[part(z_v, to=to, p=p) for p in (0, 1) for to in "mp"])
    start(part(z_m0, k=1))
    for p in (0, 1):
        arrived(part(z_v_in, to="m", p=p))
        start(part(z_vf, p=p))
    start(part(z_p0, k=1))

    first, second = pl.ds(0, 256), pl.ds(256, 256)

    def split_block(src, yy, base):
        @pl.loop(0, 2)
        def _(i):
            start_row = yy * 128 + i * 64
            to = pl.ds(pl.multiple_of(base + start_row, 64), 64)
            rh[to, :], rl[to, :] = split(src[pl.ds(pl.multiple_of(start_row, 64), 64), :])

    def product(h, lo, hi):
        for t in range(lo, hi):
            rows = pl.ds(t * 256, 256)
            ct[h, :, rows] = dot3((ph[h], plo[h]), (rh[rows, :], rl[rows, :]), NT)

    def landed(h):
        arrived(*([part(z_pe_in, e=e, h=h) for e in (1, 3, 2)] if h == 3 else [part(z_p_in, h=h)]),
                *([part(z_p0_in, k=0)] if h == 0 else [part(z_p0_in, k=1)] if h == 3 else []))

        @pl.loop(0, 4)
        def _(e):
            rows = pl.ds(pl.multiple_of(e * 64, 64), 64)
            ph[h, rows, :], plo[h, rows, :] = split(pk[h, e].reshape(64, W))

    def early(h):
        panel = pl.ds(pl.multiple_of(1024 + zl * 256, 256), 256)
        bt[h] = dot3((ph[h], plo[h]), (rh[panel, :], rl[panel, :]), NT)
        go(remote(("cb", h), bt.at[h, :, lanes(1 - c, 128)], cb.at[h], other))
        product(h, 0, 2)
        copy = remote(("cc", h), ct.at[h, :, pl.ds(0, 512)], cc.at[h], other)

        @pl.when(jnp.logical_not(home))
        def _():
            copy.start()

        away_sends.append(copy)

    def along_x(name, h, src, dst):
        out = []
        for f in ODD_FIRST:
            e = wrap(x + f - y + 4)
            out.append(remote((name, f, h), src.at[h, pl.ds(pl.multiple_of(e * 64, 64), 64)], dst.at[h, f - 1], xid(f)))
        return out

    def early_x(h):
        remote(("cb", h), cb.at[h], cb.at[h], other).wait_recv()
        kb[h] = bt[h, :, lanes(c, 128)] + cb[h]
        for q in along_x("xb", h, kb, bx):
            go(q)
        copies = along_x("xc", h, kc, cx)

        @pl.when(home)
        def _():
            remote(("cc", h), cc.at[h], cc.at[h], other).wait_recv()
            kc[h] = ct[h, :, pl.ds(0, 512)] + cc[h]
            for q in copies:
                q.start()

        home_sends.extend(copies)

    def late(h):
        product(h, 2, 4)
        copy = remote(("cc", h), ct.at[h, :, pl.ds(512, 512)], cc.at[h], other)

        @pl.when(home)
        def _():
            copy.start()

        home_sends.append(copy)

    def late_x(h):
        copies = along_x("xc", h, kc, cx)

        @pl.when(jnp.logical_not(home))
        def _():
            remote(("cc", h), cc.at[h], cc.at[h], other).wait_recv()
            kc[h] = ct[h, :, pl.ds(512, 512)] + cc[h]
            for q in copies:
                q.start()

        away_sends.extend(copies)

    mine = pl.ds(pl.multiple_of(wrap(x - y + 4) * 64, 64), 64)

    pair = lax.div(z, 2)
    b_slot = zl * 2 + c

    def b_copies(h):
        base = names("sbr", h, 0)
        for k in (1, 2, 3):
            names("sbr", h, k)
        return [pltpu.make_async_remote_copy(
            src_ref=sb.at[h], dst_ref=fb.at[h, :, lanes(b_slot, 128)], send_sem=ss.at[names("sbs", h, k)],
            recv_sem=rs.at[base + b_slot], device_id=(x * 2 + pair, y * 4 + wrap(z + k)), device_id_type=MESH)
            for k in range(4)]

    def finish_b(h):
        for f in ODD_FIRST:
            remote(("xb", f, h), bx.at[h, f - 1], bx.at[h, f - 1], xid(f)).wait_recv()
        sb[h] = (kb[h, mine, :] + bx[h, 0]) + (bx[h, 1] + bx[h, 2])
        copies = b_copies(h)
        for q in copies[1:]:
            go(q)

        @pl.when(home)
        def _():
            fb[h, :, lanes(b_slot, 128)] = sb[h]

        @pl.when(jnp.logical_not(home))
        def _():
            copies[0].start()

        away_sends.append(copies[0])

    def finish_c(h):
        for f in ODD_FIRST:
            remote(("xc", f, h), cx.at[h, f - 1], cx.at[h, f - 1], xid(f)).wait_recv()
        total = (kc[h, mine, :] + cx[h, 0]) + (cx[h, 1] + cx[h, 2])
        copy = remote(("sc", h), sc.at[h], fc.at[h], swap_mate)

        @pl.when(home)
        def _():
            fc[h] = total

        @pl.when(jnp.logical_not(home))
        def _():
            sc[h] = total
            copy.start()

        away_sends.append(copy)

    def final_b(h):
        for k in range(4):
            @pl.when(jnp.logical_not(jnp.logical_and(home, b_slot == k)))
            def _():
                ref = fb.at[h, :, pl.ds(k * 128, 128)]
                remote(("sbr", h, k), ref, ref, other).wait_recv()

        fbs = split(fb[h])
        for cols in (first, second):
            dt[h, :, cols] = dot3(fbs, (wh[cols, :], wl[cols, :]), NT)

    def final_c(h):
        @pl.when(jnp.logical_not(home))
        def _():
            remote(("sc", h), fc.at[h], fc.at[h], swap_mate).wait_recv()

        dt[h] = fc[h] - dt[h]
        for d in ODD_FIRST:
            go(remote(("cy", d, h), dt.at[h, :, lanes(wrap(y + d), 128)], cy.at[h, d - 1], yid(d)))

    def final(h):
        final_b(h)
        final_c(h)

    def done(h):
        for d in ODD_FIRST:
            remote(("cy", d, h), cy.at[h, d - 1], cy.at[h, d - 1], yid(d)).wait_recv()
        res = ((dt[h, :, lanes(y, 128)] + cy[h, 0]) + (cy[h, 1] + cy[h, 2])) / N
        of[pl.ds(h * 32, 32), :] = res[:32]
        of[pl.ds(128 + h * 32, 32), :] = res[32:]

    split_block(mk, y, 0)
    for e in (1, 3, 2):
        arrived(part(y_m_in, d=4 - e))
        start(part(z_m, e=e))
        split_block(mk, wrap(y + e), 0)
    arrived(*[part(z_v_in, to="p", p=p) for p in (0, 1)], *[part(z_vf_in, p=p) for p in (0, 1)])

    @pl.loop(0, 8)
    def _(i):
        p, yy = lax.div(i, 4), lax.rem(i, 4)
        rows = pl.ds(pl.multiple_of(1024 + i * 64, 64), 64)
        rh[rows, :], rl[rows, :] = split(vk[p, yy].reshape(64, W))

    v1s, v2s = pl.ds(1024, 256), pl.ds(1280, 256)
    gram = dot3((rh[v1s, :], rl[v1s, :]), (rh[v2s, :], rl[v2s, :]), NT)
    at[:, pl.ds(32, 8), first] = gram[:128].reshape(16, 8, 256)
    at[:, pl.ds(32, 8), second] = gram[128:].reshape(16, 8, 256)
    for t in (0, 1):
        rows = pl.ds(t * 256, 256)
        for j, cols in ((0, first), (1, second)):
            vrows = pl.ds(1024 + j * 256, 256)
            res = dot3((rh[rows, :], rl[rows, :]), (rh[vrows, :], rl[vrows, :]), NT)
            at[pl.ds(t * 8, 8), pl.ds(0, 32), cols] = res.reshape(8, 32, 256)

    core_sum = go(remote(("ac",), at.at[pl.ds((1 - c) * 8, 8)], ac, other))
    z_panel(0)
    core_sum.wait_recv()
    for k in range(8):
        at[c * 8 + k] = at[c * 8 + k] + ac[k]
    a0, b0 = c * 8, c * 8 + 4
    one = [go(remote(("ax", d), at.at[a0 + wrap(x + d)], ax.at[d - 1], xid(d))) for d in ODD_FIRST]
    one += [go(remote(("by", d), at.at[b0 + wrap(y + d)], by_.at[d - 1], yid(d))) for d in ODD_FIRST]
    y_panel(2)
    z_panel(1)
    for q in one:
        q.wait_recv()
    as_[0] = (at[a0 + x] + ax[0]) + (ax[1] + ax[2])
    as_[1] = (at[b0 + y] + by_[0]) + (by_[1] + by_[2])
    two = [go(remote(("ay", d), as_.at[0], ay.at[d - 1], yid(d))) for d in ODD_FIRST]
    two += [go(remote(("bx", d), as_.at[1], bx_.at[d - 1], xid(d))) for d in ODD_FIRST]

    y_panel(3, (1, 3))
    landed(0)
    early(0)
    early_x(0)
    z_panel(2)
    for q in two:
        q.wait_recv()
    af[a0 + x] = (as_[0] + ay[0]) + (ay[1] + ay[2])
    af[b0 + y] = (as_[1] + bx_[0]) + (bx_[1] + bx_[2])
    for d in ODD_FIRST:
        go(remote(("cx", d), af.at[a0 + x], af.at[a0 + x], xid(d)))
        go(remote(("dy", d), af.at[b0 + y], af.at[b0 + y], yid(d)))
    y_panel(3, (2,))
    landed(1)
    early(1)
    early_x(1)

    def modes_landed():
        arrived(part(z_m0_in, k=0), part(z_m0_in, k=1))
        split_block(mp, y, 512)
        for e in (1, 3, 2):
            rows = mrow(wrap(y + e))
            both(lambda n: remote(("zm", e), mp.at[rows, pl.ds(0, n * 128)], mp.at[rows, pl.ds(0, n * 128)],
                                  m_mate).wait_recv())
            split_block(mp, wrap(y + e), 512)

    def z_last(*es):
        arrived(*[part(y_p_in, d=4 - e, h=3) for e in es])
        start(*[part(z_pe, e=e, h=3) for e in es])

    modes_landed()
    late(0)
    for d in ODD_FIRST:
        ref = af.at[a0 + wrap(x + 4 - d)]
        remote(("cx", d), ref, ref, xid(d)).wait_recv()
        ref = af.at[b0 + wrap(y + 4 - d)]
        remote(("dy", d), ref, ref, yid(d)).wait_recv()
    ref = af.at[pl.ds(c * 8, 8)]
    go(remote(("bc",), ref, ref, other))
    late_x(0)
    late(1)
    ref = af.at[pl.ds((1 - c) * 8, 8)]
    remote(("bc",), ref, ref, other).wait_recv()
    z_last(1, 3)

    gram = jnp.concatenate([af[:, pl.ds(32, 8), first].reshape(128, 256),
                            af[:, pl.ds(32, 8), second].reshape(128, 256)], axis=0)
    gram2, f1s, f2s = split(gram), split(f1[...]), split(f2[...])
    for t in (0, 1):
        rows = pl.ds(t * 256, 256)
        a1 = af[pl.ds(t * 8, 8), pl.ds(0, 32), first].reshape(256, 256)
        a2 = af[pl.ds(t * 8, 8), pl.ds(0, 32), second].reshape(256, 256)
        w2 = split(dot3(split(a2), f2s, NT))
        wh[rows, second], wl[rows, second] = w2
        w1 = split(dot3(split(a1 - dot3(w2, gram2, NT)), f1s, NT))
        wh[rows, first], wl[rows, first] = w1

    vall = pl.ds(1024, 512)

    def move(d):
        rows = mrow(wrap(y + d))
        for k in range(2):
            cols = pl.ds(k * 512, 512)
            mv[rows, cols] = mk[rows, cols] - dot3((wh[rows, :], wl[rows, :]), (rh[vall, cols], rl[vall, cols]), NN)

    def own_r(n):
        return pltpu.make_async_copy(mv.at[mrow(y), pl.ds(0, n * 128)], out_m.at[:, quarter(y, n)], ls.at[4])

    late_x(1)
    move(1)
    start(part(y_r, d=1, half=0))
    move(3)
    start(part(y_r, d=3, half=0))
    z_last(2)
    landed(2)
    early(2)
    move(2)
    start(part(y_r, d=2, half=0))
    early_x(2)
    late(2)
    move(0)
    both(lambda n: own_r(n).start())
    late_x(2)
    start(*[part(y_r, d=d, half=1) for d in ODD_FIRST])
    finish_b(0)
    finish_b(1)
    landed(3)
    late(3)
    early(3)
    late_x(3)
    early_x(3)
    finish_c(0)
    finish_c(1)
    finish_b(2)
    final(0)
    finish_c(2)
    final(1)
    finish_b(3)
    finish_c(3)
    final(2)
    final_b(3)
    final_c(3)
    drain()
    done(0)
    done(1)
    done(2)
    done(3)
    out_c[...] = of[...].T

    arrived(*[part(y_r_in, d=d, half=half) for half in (0, 1) for d in ODD_FIRST])
    both(lambda n: own_r(n).wait())
    assert len(names.ids) <= SEMS, len(names.ids)


SEMS = 192


def shards(modes, prev_modes, first_vectors, first_factor, second_vectors, second_factor):
    any_, vmem = pl.BlockSpec(memory_space=pl.ANY), pl.BlockSpec(memory_space=pltpu.VMEM)
    V = pltpu.VMEM
    dma = pltpu.SemaphoreType.DMA
    return pl.pallas_call(
        kernel,
        out_shape=(jax.ShapeDtypeStruct((128, 3840), F32), jax.ShapeDtypeStruct((128, 256), F32)),
        in_specs=[any_, any_, any_, any_, vmem, vmem],
        out_specs=(any_, vmem),
        scratch_shapes=[
            V((512, W), F32), V((512, W), F32), V((512, W), F32), V((4, 4, 2, 32, W), F32), V((2, 4, 4, 16, W), F32),
            V((1536, W), BF16), V((1536, W), BF16), V((4, 256, W), BF16), V((4, 256, W), BF16),
            V((16, 40, 512), F32), V((8, 40, 512), F32), V((3, 40, 512), F32), V((3, 40, 512), F32),
            V((3, 40, 512), F32), V((3, 40, 512), F32), V((2, 40, 512), F32), V((16, 40, 512), F32),
            V((512, 512), BF16), V((512, 512), BF16),
            V((4, 256, 1024), F32), V((4, 256, 256), F32), V((4, 256, 512), F32), V((4, 256, 128), F32),
            V((4, 256, 512), F32), V((4, 256, 128), F32), V((4, 3, 64, 512), F32), V((4, 3, 64, 128), F32),
            V((4, 64, 512), F32), V((4, 64, 128), F32), V((4, 64, 512), F32), V((4, 64, 512), F32),
            V((4, 64, 512), F32), V((4, 3, 64, 128), F32), V((256, 128), F32),
            dma((SEMS,)), dma((SEMS,)), dma((5,)),
        ],
        compiler_params=pltpu.CompilerParams(
            collective_id=0, has_side_effects=True, vmem_limit_bytes=60 * 2**20),
        name="reflect_and_correlate",
    )(modes, prev_modes.reshape(4, 32, 3840), first_vectors, second_vectors, first_factor, second_factor)


def solution(mesh):
    in_specs = (P("col", "row"), P("col", "row"), P("col", "row"), P(), P("col", "row"), P())
    out_specs = (P("col", "row"), P("col", "row"))
    return jax.shard_map(shards, mesh=mesh, in_specs=in_specs, out_specs=out_specs, check_vma=False)
```

```python
import functools

import jax
import jax.numpy as jnp
from jax import lax
from jax.experimental import pallas as pl
from jax.experimental.pallas import tpu as pltpu
from jax.sharding import PartitionSpec as P

N = 30720
MESH = pl.DeviceIdType.MESH
F32 = jnp.float32
BF16 = jnp.bfloat16
W = 1024
ODD_FIRST = (1, 3, 2)


def split(value):
    high = value.astype(BF16)
    return high, (value - high.astype(F32)).astype(BF16)


def dot3(left, right, dims):
    (lh, ll), (rh, rl) = left, right
    mul = functools.partial(lax.dot_general, dimension_numbers=(dims, ((), ())), preferred_element_type=F32)
    return mul(lh, rh) + (mul(lh, rl) + mul(ll, rh))


NT = ((1,), (1,))
NN = ((1,), (0,))


class Names:
    def __init__(self):
        self.ids = {}

    def __call__(self, *name):
        return self.ids.setdefault(name, len(self.ids))


def kernel(m_in, p_in, v1_in, v2_in, f1, f2, out_m, out_c,
           mk, mp, mv, pk, vk, rh, rl, ph, plo, at, ac, ax, ay, bx_, by_, as_, af, wh, wl,
           ct, bt, cc, cb, kc, kb, cx, bx, sc, sb, fc, fb, dt, cy, ss, rs, ls):
    r, col = lax.axis_index("row"), lax.axis_index("col")
    x, c = lax.div(r, 2), lax.rem(r, 2)
    y, z = lax.div(col, 4), lax.rem(col, 4)
    eight = lax.rem(y + c, 2) == 0
    home = c == lax.div(z, 2)
    zl = lax.rem(z, 2)

    def wrap(a):
        return lax.rem(a, 4)

    def yid(d):
        return (r, wrap(y + d) * 4 + z)

    def zid(d):
        return (r, y * 4 + wrap(z + d))

    def xid(d):
        return (wrap(x + d) * 2 + c, col)

    other = (x * 2 + 1 - c, col)
    p_mate = (r, y * 4 + z + 1 - 2 * zl)
    m_mate = (r, y * 4 + 3 - z)
    swap_mate = (x * 2 + 1 - c, y * 4 + 3 - z)
    names = Names()

    def both(fn):
        @pl.when(eight)
        def _():
            fn(8)

        @pl.when(jnp.logical_not(eight))
        def _():
            fn(7)

    def remote(name, src, dst, dev):
        i = names(*name)
        return pltpu.make_async_remote_copy(
            src_ref=src, dst_ref=dst, send_sem=ss.at[i], recv_sem=rs.at[i], device_id=dev, device_id_type=MESH)

    def quarter(q, n):
        start = 15 * lax.div(q, 2) + lax.rem(q, 2) * (8 - c)
        return pl.ds(pl.multiple_of(start * 128, 128), n * 128)

    def width(n, d):
        return 15 - n if d % 2 else n

    def mrow(yy, first=0, count=128):
        return pl.ds(pl.multiple_of(yy * 128 + first, 32), count)

    def lanes(i, step):
        return pl.ds(pl.multiple_of(i * step, step), step)

    sends = []
    fixed = []
    home_sends, away_sends = [], []

    def y_v(n, d, p):
        nd, q = width(n, d), wrap(y + d)
        src = (v1_in, v2_in)[p]
        return remote(("yv", d, p), src.at[:, quarter(q, nd)], vk.at[p, y, z, :, pl.ds(0, nd * 128)], yid(d))

    def y_v_in(n, d, p):
        dst = vk.at[p, wrap(y + 4 - d), z, :, pl.ds(0, n * 128)]
        return remote(("yv", d, p), dst, dst, yid(d))

    def y_m(n, d):
        nd, q = width(n, d), wrap(y + d)
        return remote(("ym", d), m_in.at[:, quarter(q, nd)], mk.at[mrow(y), pl.ds(0, nd * 128)], yid(d))

    def y_m_in(n, d):
        dst = mk.at[mrow(wrap(y + 4 - d)), pl.ds(0, n * 128)]
        return remote(("ym", d), dst, dst, yid(d))

    def y_p(n, d, h):
        nd, q = width(n, d), wrap(y + d)
        return remote(("yp", d, h), p_in.at[h, :, quarter(q, nd)], pk.at[h, 4 - d, zl, :, pl.ds(0, nd * 128)], yid(d))

    def y_p_in(n, d, h):
        dst = pk.at[h, 4 - d, zl, :, pl.ds(0, n * 128)]
        return remote(("yp", d, h), dst, dst, yid(d))

    def z_v(n, to, p):
        ref = vk.at[p, :, z, :, pl.ds(0, n * 128)]
        return remote(("zv", to, p), ref, ref, p_mate if to == "p" else m_mate)

    def z_v_in(n, to, p):
        ref = vk.at[p, :, (z + 1 - 2 * zl) if to == "p" else 3 - z, :, pl.ds(0, n * 128)]
        return remote(("zv", to, p), ref, ref, p_mate)

    def z_vf(n, p):
        ref = vk.at[p, :, 3 - z, :, pl.ds(0, n * 128)]
        return remote(("zvf", p), ref, ref, p_mate)

    def z_vf_in(n, p):
        ref = vk.at[p, :, wrap(z + 2), :, pl.ds(0, n * 128)]
        return remote(("zvf", p), ref, ref, p_mate)

    def z_m0(n, k):
        a, b = ((0, 96), (96, 32))[k]
        return remote(("zm0", k), m_in.at[pl.ds(a, b), quarter(y, n)], mp.at[mrow(y, a, b), pl.ds(0, n * 128)], m_mate)

    def z_m0_in(n, k):
        a, b = ((0, 96), (96, 32))[k]
        ref = mp.at[mrow(y, a, b), pl.ds(0, n * 128)]
        return remote(("zm0", k), ref, ref, m_mate)

    def z_m(n, e):
        rows = mrow(wrap(y + e))
        return remote(("zm", e), mk.at[rows, pl.ds(0, n * 128)], mp.at[rows, pl.ds(0, n * 128)], m_mate)

    def z_p0(n, k):
        a, b = ((0, 3), (3, 1))[k]
        return remote(("zp0", k), p_in.at[pl.ds(a, b), :, quarter(y, n)],
                      pk.at[pl.ds(a, b), 0, zl, :, pl.ds(0, n * 128)], p_mate)

    def z_p0_in(n, k):
        a, b = ((0, 3), (3, 1))[k]
        ref = pk.at[pl.ds(a, b), 0, 1 - zl, :, pl.ds(0, n * 128)]
        return remote(("zp0", k), ref, ref, p_mate)

    def z_p(n, h):
        ref = pk.at[h, pl.ds(1, 3), zl, :, pl.ds(0, n * 128)]
        return remote(("zp", h), ref, ref, p_mate)

    def z_pe(n, e, h):
        ref = pk.at[h, e, zl, :, pl.ds(0, n * 128)]
        return remote(("zpe", e, h), ref, ref, p_mate)

    def z_pe_in(n, e, h):
        ref = pk.at[h, e, 1 - zl, :, pl.ds(0, n * 128)]
        return remote(("zpe", e, h), ref, ref, p_mate)

    def z_p_in(n, h):
        ref = pk.at[h, pl.ds(1, 3), 1 - zl, :, pl.ds(0, n * 128)]
        return remote(("zp", h), ref, ref, p_mate)

    def y_r(n, d, half):
        return remote(("yr", d, half), mv.at[mrow(wrap(y + d), half * 64, 64), pl.ds(0, n * 128)],
                      out_m.at[pl.ds(half * 64, 64), quarter(y, n)], yid(d))

    def y_r_in(n, d, half):
        dst = out_m.at[pl.ds(half * 64, 64), quarter(wrap(y + 4 - d), width(n, d))]
        return remote(("yr", d, half), dst, dst, yid(d))

    def start(*fns):
        both(lambda n: [f(n).start() for f in fns] and None)
        sends.extend(fns)

    def arrived(*fns):
        both(lambda n: [f(n).wait_recv() for f in fns] and None)

    def go(copy):
        copy.start()
        fixed.append(copy)
        return copy

    part = functools.partial

    def drain():
        widths, plain, here, there = list(sends), list(fixed), list(home_sends), list(away_sends)
        both(lambda n: [f(n).wait_send() for f in widths] and None)
        for copy in plain:
            copy.wait_send()

        @pl.when(home)
        def _():
            for copy in here:
                copy.wait_send()

        @pl.when(jnp.logical_not(home))
        def _():
            for copy in there:
                copy.wait_send()

        for held in (sends, fixed, home_sends, away_sends):
            held.clear()

    @pl.when(jnp.logical_not(eight))
    def _():
        pad = pl.ds(896, 128)
        mk[:, pad] = jnp.zeros((512, 128), F32)
        mp[:, pad] = jnp.zeros((512, 128), F32)
        pk[:, :, :, :, pad] = jnp.zeros((4, 4, 2, 32, 128), F32)
        vk[:, :, :, :, pad] = jnp.zeros((2, 4, 4, 16, 128), F32)

    barrier = pltpu.get_barrier_semaphore()
    peers = [yid(1), yid(2), yid(3), xid(1), xid(2), xid(3), other, zid(1), zid(2), zid(3)]
    peers += [(x * 2 + 1 - c, y * 4 + wrap(z + d)) for d in (1, 2, 3)]
    for dev in peers:
        pl.semaphore_signal(barrier, inc=1, device_id=dev, device_id_type=MESH)
    pl.semaphore_wait(barrier, len(peers))

    start(*[part(y_v, d=d, p=p) for d in ODD_FIRST for p in (0, 1)])
    start(part(z_p0, k=0), part(z_m0, k=0))

    def own(n):
        return [
            pltpu.make_async_copy(v1_in.at[:, quarter(y, n)], vk.at[0, y, z, :, pl.ds(0, n * 128)], ls.at[0]),
            pltpu.make_async_copy(v2_in.at[:, quarter(y, n)], vk.at[1, y, z, :, pl.ds(0, n * 128)], ls.at[1]),
            pltpu.make_async_copy(m_in.at[:, quarter(y, n)], mk.at[mrow(y), pl.ds(0, n * 128)], ls.at[2]),
            pltpu.make_async_copy(p_in.at[:, :, quarter(y, n)], pk.at[:, 0, zl, :, pl.ds(0, n * 128)], ls.at[3]),
        ]

    both(lambda n: [q.start() for q in own(n)] and None)

    def y_panel(h, ds=ODD_FIRST):
        start(*[part(y_p, d=d, h=h) for d in ds])

    def z_panel(h):
        arrived(*[part(y_p_in, d=d, h=h) for d in ODD_FIRST])
        start(part(z_p, h=h))

    start(*[part(y_m, d=d) for d in ODD_FIRST])
    y_panel(0)
    y_panel(1)

    arrived(*[part(y_v_in, d=d, p=p) for d in ODD_FIRST for p in (0, 1)])
    both(lambda n: [q.wait() for q in own(n)] and None)
    start(*[part(z_v, to=to, p=p) for p in (0, 1) for to in "mp"])
    start(part(z_m0, k=1))
    for p in (0, 1):
        arrived(part(z_v_in, to="m", p=p))
        start(part(z_vf, p=p))
    start(part(z_p0, k=1))

    first, second = pl.ds(0, 256), pl.ds(256, 256)

    def split_block(src, yy, base):
        @pl.loop(0, 2)
        def _(i):
            start_row = yy * 128 + i * 64
            to = pl.ds(pl.multiple_of(base + start_row, 64), 64)
            rh[to, :], rl[to, :] = split(src[pl.ds(pl.multiple_of(start_row, 64), 64), :])

    def product(h, lo, hi):
        for t in range(lo, hi):
            rows = pl.ds(t * 256, 256)
            ct[h, :, rows] = dot3((ph[h], plo[h]), (rh[rows, :], rl[rows, :]), NT)

    def landed(h):
        arrived(*([part(z_pe_in, e=e, h=h) for e in (1, 3, 2)] if h == 3 else [part(z_p_in, h=h)]),
                *([part(z_p0_in, k=0)] if h == 0 else [part(z_p0_in, k=1)] if h == 3 else []))

        @pl.loop(0, 4)
        def _(e):
            rows = pl.ds(pl.multiple_of(e * 64, 64), 64)
            ph[h, rows, :], plo[h, rows, :] = split(pk[h, e].reshape(64, W))

    def early(h):
        panel = pl.ds(pl.multiple_of(1024 + zl * 256, 256), 256)
        bt[h] = dot3((ph[h], plo[h]), (rh[panel, :], rl[panel, :]), NT)
        go(remote(("cb", h), bt.at[h, :, lanes(1 - c, 128)], cb.at[h], other))
        product(h, 0, 2)
        copy = remote(("cc", h), ct.at[h, :, pl.ds(0, 512)], cc.at[h], other)

        @pl.when(jnp.logical_not(home))
        def _():
            copy.start()

        away_sends.append(copy)

    def along_x(name, h, src, dst):
        out = []
        for f in ODD_FIRST:
            e = wrap(x + f - y + 4)
            out.append(remote((name, f, h), src.at[h, pl.ds(pl.multiple_of(e * 64, 64), 64)], dst.at[h, f - 1], xid(f)))
        return out

    def early_x(h):
        remote(("cb", h), cb.at[h], cb.at[h], other).wait_recv()
        kb[h] = bt[h, :, lanes(c, 128)] + cb[h]
        for q in along_x("xb", h, kb, bx):
            go(q)
        copies = along_x("xc", h, kc, cx)

        @pl.when(home)
        def _():
            remote(("cc", h), cc.at[h], cc.at[h], other).wait_recv()
            kc[h] = ct[h, :, pl.ds(0, 512)] + cc[h]
            for q in copies:
                q.start()

        home_sends.extend(copies)

    def late(h):
        product(h, 2, 4)
        copy = remote(("cc", h), ct.at[h, :, pl.ds(512, 512)], cc.at[h], other)

        @pl.when(home)
        def _():
            copy.start()

        home_sends.append(copy)

    def late_x(h):
        copies = along_x("xc", h, kc, cx)

        @pl.when(jnp.logical_not(home))
        def _():
            remote(("cc", h), cc.at[h], cc.at[h], other).wait_recv()
            kc[h] = ct[h, :, pl.ds(512, 512)] + cc[h]
            for q in copies:
                q.start()

        away_sends.extend(copies)

    mine = pl.ds(pl.multiple_of(wrap(x - y + 4) * 64, 64), 64)

    pair = lax.div(z, 2)
    b_slot = zl * 2 + c

    def b_copies(h):
        base = names("sbr", h, 0)
        for k in (1, 2, 3):
            names("sbr", h, k)
        return [pltpu.make_async_remote_copy(
            src_ref=sb.at[h], dst_ref=fb.at[h, :, lanes(b_slot, 128)], send_sem=ss.at[names("sbs", h, k)],
            recv_sem=rs.at[base + b_slot], device_id=(x * 2 + pair, y * 4 + wrap(z + k)), device_id_type=MESH)
            for k in range(4)]

    def finish_b(h):
        for f in ODD_FIRST:
            remote(("xb", f, h), bx.at[h, f - 1], bx.at[h, f - 1], xid(f)).wait_recv()
        sb[h] = (kb[h, mine, :] + bx[h, 0]) + (bx[h, 1] + bx[h, 2])
        copies = b_copies(h)
        for q in copies[1:]:
            go(q)

        @pl.when(home)
        def _():
            fb[h, :, lanes(b_slot, 128)] = sb[h]

        @pl.when(jnp.logical_not(home))
        def _():
            copies[0].start()

        away_sends.append(copies[0])

    def finish_c(h):
        for f in ODD_FIRST:
            remote(("xc", f, h), cx.at[h, f - 1], cx.at[h, f - 1], xid(f)).wait_recv()
        total = (kc[h, mine, :] + cx[h, 0]) + (cx[h, 1] + cx[h, 2])
        copy = remote(("sc", h), sc.at[h], fc.at[h], swap_mate)

        @pl.when(home)
        def _():
            fc[h] = total

        @pl.when(jnp.logical_not(home))
        def _():
            sc[h] = total
            copy.start()

        away_sends.append(copy)

    def final_b(h):
        for k in range(4):
            @pl.when(jnp.logical_not(jnp.logical_and(home, b_slot == k)))
            def _():
                ref = fb.at[h, :, pl.ds(k * 128, 128)]
                remote(("sbr", h, k), ref, ref, other).wait_recv()

        fbs = split(fb[h])
        for cols in (first, second):
            dt[h, :, cols] = dot3(fbs, (wh[cols, :], wl[cols, :]), NT)

    def final_c(h):
        @pl.when(jnp.logical_not(home))
        def _():
            remote(("sc", h), fc.at[h], fc.at[h], swap_mate).wait_recv()

        dt[h] = fc[h] - dt[h]
        for d in ODD_FIRST:
            go(remote(("cy", d, h), dt.at[h, :, lanes(wrap(y + d), 128)], cy.at[h, d - 1], yid(d)))

    def final(h):
        final_b(h)
        final_c(h)

    def done(h):
        for d in ODD_FIRST:
            remote(("cy", d, h), cy.at[h, d - 1], cy.at[h, d - 1], yid(d)).wait_recv()
        res = ((dt[h, :, lanes(y, 128)] + cy[h, 0]) + (cy[h, 1] + cy[h, 2])) / N
        out_c[pl.ds(h * 32, 32), :] = res[:32]
        out_c[pl.ds(128 + h * 32, 32), :] = res[32:]

    split_block(mk, y, 0)
    for e in (1, 3, 2):
        arrived(part(y_m_in, d=4 - e))
        start(part(z_m, e=e))
        split_block(mk, wrap(y + e), 0)
    arrived(*[part(z_v_in, to="p", p=p) for p in (0, 1)], *[part(z_vf_in, p=p) for p in (0, 1)])

    @pl.loop(0, 8)
    def _(i):
        p, yy = lax.div(i, 4), lax.rem(i, 4)
        rows = pl.ds(pl.multiple_of(1024 + i * 64, 64), 64)
        rh[rows, :], rl[rows, :] = split(vk[p, yy].reshape(64, W))

    v1s, v2s = pl.ds(1024, 256), pl.ds(1280, 256)
    gram = dot3((rh[v1s, :], rl[v1s, :]), (rh[v2s, :], rl[v2s, :]), NT)
    at[:, pl.ds(32, 8), first] = gram[:128].reshape(16, 8, 256)
    at[:, pl.ds(32, 8), second] = gram[128:].reshape(16, 8, 256)
    for t in (0, 1):
        rows = pl.ds(t * 256, 256)
        for j, cols in ((0, first), (1, second)):
            vrows = pl.ds(1024 + j * 256, 256)
            res = dot3((rh[rows, :], rl[rows, :]), (rh[vrows, :], rl[vrows, :]), NT)
            at[pl.ds(t * 8, 8), pl.ds(0, 32), cols] = res.reshape(8, 32, 256)

    core_sum = go(remote(("ac",), at.at[pl.ds((1 - c) * 8, 8)], ac, other))
    z_panel(0)
    core_sum.wait_recv()
    for k in range(8):
        at[c * 8 + k] = at[c * 8 + k] + ac[k]
    a0, b0 = c * 8, c * 8 + 4
    one = [go(remote(("ax", d), at.at[a0 + wrap(x + d)], ax.at[d - 1], xid(d))) for d in ODD_FIRST]
    one += [go(remote(("by", d), at.at[b0 + wrap(y + d)], by_.at[d - 1], yid(d))) for d in ODD_FIRST]
    y_panel(2)
    z_panel(1)
    for q in one:
        q.wait_recv()
    as_[0] = (at[a0 + x] + ax[0]) + (ax[1] + ax[2])
    as_[1] = (at[b0 + y] + by_[0]) + (by_[1] + by_[2])
    two = [go(remote(("ay", d), as_.at[0], ay.at[d - 1], yid(d))) for d in ODD_FIRST]
    two += [go(remote(("bx", d), as_.at[1], bx_.at[d - 1], xid(d))) for d in ODD_FIRST]

    y_panel(3, (1, 3))
    landed(0)
    early(0)
    early_x(0)
    z_panel(2)
    for q in two:
        q.wait_recv()
    af[a0 + x] = (as_[0] + ay[0]) + (ay[1] + ay[2])
    af[b0 + y] = (as_[1] + bx_[0]) + (bx_[1] + bx_[2])
    for d in ODD_FIRST:
        go(remote(("cx", d), af.at[a0 + x], af.at[a0 + x], xid(d)))
        go(remote(("dy", d), af.at[b0 + y], af.at[b0 + y], yid(d)))
    y_panel(3, (2,))
    landed(1)
    early(1)
    early_x(1)

    def modes_landed():
        arrived(part(z_m0_in, k=0), part(z_m0_in, k=1))
        split_block(mp, y, 512)
        for e in (1, 3, 2):
            rows = mrow(wrap(y + e))
            both(lambda n: remote(("zm", e), mp.at[rows, pl.ds(0, n * 128)], mp.at[rows, pl.ds(0, n * 128)],
                                  m_mate).wait_recv())
            split_block(mp, wrap(y + e), 512)

    def z_last(*es):
        arrived(*[part(y_p_in, d=4 - e, h=3) for e in es])
        start(*[part(z_pe, e=e, h=3) for e in es])

    modes_landed()
    late(0)
    for d in ODD_FIRST:
        ref = af.at[a0 + wrap(x + 4 - d)]
        remote(("cx", d), ref, ref, xid(d)).wait_recv()
        ref = af.at[b0 + wrap(y + 4 - d)]
        remote(("dy", d), ref, ref, yid(d)).wait_recv()
    ref = af.at[pl.ds(c * 8, 8)]
    go(remote(("bc",), ref, ref, other))
    late_x(0)
    late(1)
    ref = af.at[pl.ds((1 - c) * 8, 8)]
    remote(("bc",), ref, ref, other).wait_recv()
    z_last(1, 3)

    gram = jnp.concatenate([af[:, pl.ds(32, 8), first].reshape(128, 256),
                            af[:, pl.ds(32, 8), second].reshape(128, 256)], axis=0)
    gram2, f1s, f2s = split(gram), split(f1[...]), split(f2[...])
    for t in (0, 1):
        rows = pl.ds(t * 256, 256)
        a1 = af[pl.ds(t * 8, 8), pl.ds(0, 32), first].reshape(256, 256)
        a2 = af[pl.ds(t * 8, 8), pl.ds(0, 32), second].reshape(256, 256)
        w2 = split(dot3(split(a2), f2s, NT))
        wh[rows, second], wl[rows, second] = w2
        w1 = split(dot3(split(a1 - dot3(w2, gram2, NT)), f1s, NT))
        wh[rows, first], wl[rows, first] = w1

    vall = pl.ds(1024, 512)

    def move(d):
        rows = mrow(wrap(y + d))
        for k in range(2):
            cols = pl.ds(k * 512, 512)
            mv[rows, cols] = mk[rows, cols] - dot3((wh[rows, :], wl[rows, :]), (rh[vall, cols], rl[vall, cols]), NN)

    def own_r(n):
        return pltpu.make_async_copy(mv.at[mrow(y), pl.ds(0, n * 128)], out_m.at[:, quarter(y, n)], ls.at[4])

    late_x(1)
    move(1)
    start(part(y_r, d=1, half=0))
    move(3)
    start(part(y_r, d=3, half=0))
    z_last(2)
    landed(2)
    early(2)
    move(2)
    start(part(y_r, d=2, half=0))
    early_x(2)
    late(2)
    move(0)
    both(lambda n: own_r(n).start())
    late_x(2)
    start(*[part(y_r, d=d, half=1) for d in ODD_FIRST])
    finish_b(0)
    finish_b(1)
    landed(3)
    late(3)
    early(3)
    late_x(3)
    early_x(3)
    finish_c(0)
    finish_c(1)
    finish_b(2)
    final(0)
    finish_c(2)
    final(1)
    finish_b(3)
    finish_c(3)
    final(2)
    final_b(3)
    final_c(3)
    drain()
    done(0)
    done(1)
    done(2)
    done(3)

    arrived(*[part(y_r_in, d=d, half=half) for half in (0, 1) for d in ODD_FIRST])
    both(lambda n: own_r(n).wait())
    assert len(names.ids) <= SEMS, len(names.ids)


SEMS = 192


def place(m_ref, t_ref, m_out, c_out, m_buf, t_buf, c_buf, come, go):
    rows = [pl.ds(i * 16, 16) for i in range(8)]
    reads = [pltpu.make_async_copy(t_ref, t_buf, come.at[8])]
    reads += [pltpu.make_async_copy(m_ref.at[q], m_buf.at[q], come.at[i]) for i, q in enumerate(rows)]
    writes = [pltpu.make_async_copy(c_buf, c_out, go.at[8])]
    writes += [pltpu.make_async_copy(m_buf.at[q], m_out.at[q], go.at[i]) for i, q in enumerate(rows)]
    for copy in reads:
        copy.start()
    reads[0].wait()
    c_buf[...] = t_buf[...].T
    writes[0].start()
    for come_in, go_out in zip(reads[1:], writes[1:]):
        come_in.wait()
        go_out.start()
    for copy in writes:
        copy.wait()


def shards(modes, prev_modes, first_vectors, first_factor, second_vectors, second_factor):
    any_, vmem = pl.BlockSpec(memory_space=pl.ANY), pl.BlockSpec(memory_space=pltpu.VMEM)
    V = pltpu.VMEM
    dma = pltpu.SemaphoreType.DMA
    moved, turned = pl.pallas_call(
        kernel,
        out_shape=(jax.ShapeDtypeStruct((128, 3840), F32), jax.ShapeDtypeStruct((256, 128), F32)),
        in_specs=[any_, any_, any_, any_, vmem, vmem],
        out_specs=(any_, vmem),
        scratch_shapes=[
            V((512, W), F32), V((512, W), F32), V((512, W), F32), V((4, 4, 2, 32, W), F32), V((2, 4, 4, 16, W), F32),
            V((1536, W), BF16), V((1536, W), BF16), V((4, 256, W), BF16), V((4, 256, W), BF16),
            V((16, 40, 512), F32), V((8, 40, 512), F32), V((3, 40, 512), F32), V((3, 40, 512), F32),
            V((3, 40, 512), F32), V((3, 40, 512), F32), V((2, 40, 512), F32), V((16, 40, 512), F32),
            V((512, 512), BF16), V((512, 512), BF16),
            V((4, 256, 1024), F32), V((4, 256, 256), F32), V((4, 256, 512), F32), V((4, 256, 128), F32),
            V((4, 256, 512), F32), V((4, 256, 128), F32), V((4, 3, 64, 512), F32), V((4, 3, 64, 128), F32),
            V((4, 64, 512), F32), V((4, 64, 128), F32), V((4, 64, 512), F32), V((4, 64, 512), F32),
            V((4, 64, 512), F32), V((4, 3, 64, 128), F32),
            dma((SEMS,)), dma((SEMS,)), dma((5,)),
        ],
        compiler_params=pltpu.CompilerParams(
            collective_id=0, has_side_effects=True, vmem_limit_bytes=60 * 2**20),
        name="reflect_and_correlate",
    )(modes, prev_modes.reshape(4, 32, 3840), first_vectors, second_vectors, first_factor, second_factor)
    return pl.pallas_call(
        place,
        out_shape=(jax.ShapeDtypeStruct((128, 3840), F32), jax.ShapeDtypeStruct((128, 256), F32)),
        in_specs=[any_, any_],
        out_specs=(any_, any_),
        scratch_shapes=[V((128, 3840), F32), V((256, 128), F32), V((128, 256), F32), dma((9,)), dma((9,))],
        compiler_params=pltpu.CompilerParams(vmem_limit_bytes=60 * 2**20),
        name="place",
    )(moved, turned)


def solution(mesh):
    in_specs = (P("col", "row"), P("col", "row"), P("col", "row"), P(), P("col", "row"), P())
    out_specs = (P("col", "row"), P("col", "row"))
    return jax.shard_map(shards, mesh=mesh, in_specs=in_specs, out_specs=out_specs, check_vma=False)
```

```python
import functools

import jax
import jax.numpy as jnp
from jax import lax
from jax.experimental import pallas as pl
from jax.experimental.pallas import tpu as pltpu
from jax.sharding import PartitionSpec as P

N = 30720
MESH = pl.DeviceIdType.MESH
F32 = jnp.float32
BF16 = jnp.bfloat16
W = 1024
ODD_FIRST = (1, 3, 2)


def split(value):
    high = value.astype(BF16)
    return high, (value - high.astype(F32)).astype(BF16)


def dot3(left, right, dims):
    (lh, ll), (rh, rl) = left, right
    mul = functools.partial(lax.dot_general, dimension_numbers=(dims, ((), ())), preferred_element_type=F32)
    return mul(lh, rh) + (mul(lh, rl) + mul(ll, rh))


NT = ((1,), (1,))
NN = ((1,), (0,))


class Names:
    def __init__(self):
        self.ids = {}

    def __call__(self, *name):
        return self.ids.setdefault(name, len(self.ids))


def kernel(m_in, p_in, v1_in, v2_in, f1, f2, out_m, out_c,
           mk, mp, mv, pk, vk, rh, rl, ph, plo, at, ac, ax, ay, bx_, by_, as_, af, wh, wl,
           ct, bt, cc, cb, kc, kb, cx, bx, sc, sb, fc, fb, dt, cy, ss, rs, ls):
    r, col = lax.axis_index("row"), lax.axis_index("col")
    x, c = lax.div(r, 2), lax.rem(r, 2)
    y, z = lax.div(col, 4), lax.rem(col, 4)
    eight = lax.rem(y + c, 2) == 0
    home = c == lax.div(z, 2)
    zl = lax.rem(z, 2)

    def wrap(a):
        return lax.rem(a, 4)

    def yid(d):
        return (r, wrap(y + d) * 4 + z)

    def zid(d):
        return (r, y * 4 + wrap(z + d))

    def xid(d):
        return (wrap(x + d) * 2 + c, col)

    other = (x * 2 + 1 - c, col)
    p_mate = (r, y * 4 + z + 1 - 2 * zl)
    m_mate = (r, y * 4 + 3 - z)
    swap_mate = (x * 2 + 1 - c, y * 4 + 3 - z)
    names = Names()

    def both(fn):
        @pl.when(eight)
        def _():
            fn(8)

        @pl.when(jnp.logical_not(eight))
        def _():
            fn(7)

    def remote(name, src, dst, dev):
        i = names(*name)
        return pltpu.make_async_remote_copy(
            src_ref=src, dst_ref=dst, send_sem=ss.at[i], recv_sem=rs.at[i], device_id=dev, device_id_type=MESH)

    def quarter(q, n):
        start = 15 * lax.div(q, 2) + lax.rem(q, 2) * (8 - c)
        return pl.ds(pl.multiple_of(start * 128, 128), n * 128)

    def width(n, d):
        return 15 - n if d % 2 else n

    def mrow(yy, first=0, count=128):
        return pl.ds(pl.multiple_of(yy * 128 + first, 32), count)

    def lanes(i, step):
        return pl.ds(pl.multiple_of(i * step, step), step)

    sends = []
    fixed = []
    home_sends, away_sends = [], []

    def y_v(n, d, p):
        nd, q = width(n, d), wrap(y + d)
        src = (v1_in, v2_in)[p]
        return remote(("yv", d, p), src.at[:, quarter(q, nd)], vk.at[p, y, z, :, pl.ds(0, nd * 128)], yid(d))

    def y_v_in(n, d, p):
        dst = vk.at[p, wrap(y + 4 - d), z, :, pl.ds(0, n * 128)]
        return remote(("yv", d, p), dst, dst, yid(d))

    def y_m(n, d):
        nd, q = width(n, d), wrap(y + d)
        return remote(("ym", d), m_in.at[:, quarter(q, nd)], mk.at[mrow(y), pl.ds(0, nd * 128)], yid(d))

    def y_m_in(n, d):
        dst = mk.at[mrow(wrap(y + 4 - d)), pl.ds(0, n * 128)]
        return remote(("ym", d), dst, dst, yid(d))

    def y_p(n, d, h):
        nd, q = width(n, d), wrap(y + d)
        return remote(("yp", d, h), p_in.at[h, :, quarter(q, nd)], pk.at[h, 4 - d, zl, :, pl.ds(0, nd * 128)], yid(d))

    def y_p_in(n, d, h):
        dst = pk.at[h, 4 - d, zl, :, pl.ds(0, n * 128)]
        return remote(("yp", d, h), dst, dst, yid(d))

    def z_v(n, to, p):
        ref = vk.at[p, :, z, :, pl.ds(0, n * 128)]
        return remote(("zv", to, p), ref, ref, p_mate if to == "p" else m_mate)

    def z_v_in(n, to, p):
        ref = vk.at[p, :, (z + 1 - 2 * zl) if to == "p" else 3 - z, :, pl.ds(0, n * 128)]
        return remote(("zv", to, p), ref, ref, p_mate)

    def z_vf(n, p):
        ref = vk.at[p, :, 3 - z, :, pl.ds(0, n * 128)]
        return remote(("zvf", p), ref, ref, p_mate)

    def z_vf_in(n, p):
        ref = vk.at[p, :, wrap(z + 2), :, pl.ds(0, n * 128)]
        return remote(("zvf", p), ref, ref, p_mate)

    def z_m0(n, k):
        a, b = ((0, 96), (96, 32))[k]
        return remote(("zm0", k), m_in.at[pl.ds(a, b), quarter(y, n)], mp.at[mrow(y, a, b), pl.ds(0, n * 128)], m_mate)

    def z_m0_in(n, k):
        a, b = ((0, 96), (96, 32))[k]
        ref = mp.at[mrow(y, a, b), pl.ds(0, n * 128)]
        return remote(("zm0", k), ref, ref, m_mate)

    def z_m(n, e):
        rows = mrow(wrap(y + e))
        return remote(("zm", e), mk.at[rows, pl.ds(0, n * 128)], mp.at[rows, pl.ds(0, n * 128)], m_mate)

    def z_p0(n, k):
        a, b = ((0, 3), (3, 1))[k]
        return remote(("zp0", k), p_in.at[pl.ds(a, b), :, quarter(y, n)],
                      pk.at[pl.ds(a, b), 0, zl, :, pl.ds(0, n * 128)], p_mate)

    def z_p0_in(n, k):
        a, b = ((0, 3), (3, 1))[k]
        ref = pk.at[pl.ds(a, b), 0, 1 - zl, :, pl.ds(0, n * 128)]
        return remote(("zp0", k), ref, ref, p_mate)

    def z_p(n, h):
        ref = pk.at[h, pl.ds(1, 3), zl, :, pl.ds(0, n * 128)]
        return remote(("zp", h), ref, ref, p_mate)

    def z_pe(n, e, h):
        ref = pk.at[h, e, zl, :, pl.ds(0, n * 128)]
        return remote(("zpe", e, h), ref, ref, p_mate)

    def z_pe_in(n, e, h):
        ref = pk.at[h, e, 1 - zl, :, pl.ds(0, n * 128)]
        return remote(("zpe", e, h), ref, ref, p_mate)

    def z_p_in(n, h):
        ref = pk.at[h, pl.ds(1, 3), 1 - zl, :, pl.ds(0, n * 128)]
        return remote(("zp", h), ref, ref, p_mate)

    def y_r(n, d, half):
        return remote(("yr", d, half), mv.at[mrow(wrap(y + d), half * 64, 64), pl.ds(0, n * 128)],
                      out_m.at[pl.ds(half * 64, 64), quarter(y, n)], yid(d))

    def y_r_in(n, d, half):
        dst = out_m.at[pl.ds(half * 64, 64), quarter(wrap(y + 4 - d), width(n, d))]
        return remote(("yr", d, half), dst, dst, yid(d))

    def start(*fns):
        both(lambda n: [f(n).start() for f in fns] and None)
        sends.extend(fns)

    def arrived(*fns):
        both(lambda n: [f(n).wait_recv() for f in fns] and None)

    def go(copy):
        copy.start()
        fixed.append(copy)
        return copy

    part = functools.partial

    def drain():
        widths, plain, here, there = list(sends), list(fixed), list(home_sends), list(away_sends)
        both(lambda n: [f(n).wait_send() for f in widths] and None)
        for copy in plain:
            copy.wait_send()

        @pl.when(home)
        def _():
            for copy in here:
                copy.wait_send()

        @pl.when(jnp.logical_not(home))
        def _():
            for copy in there:
                copy.wait_send()

        for held in (sends, fixed, home_sends, away_sends):
            held.clear()

    @pl.when(jnp.logical_not(eight))
    def _():
        pad = pl.ds(896, 128)
        mk[:, pad] = jnp.zeros((512, 128), F32)
        mp[:, pad] = jnp.zeros((512, 128), F32)
        pk[:, :, :, :, pad] = jnp.zeros((4, 4, 2, 32, 128), F32)
        vk[:, :, :, :, pad] = jnp.zeros((2, 4, 4, 16, 128), F32)

    barrier = pltpu.get_barrier_semaphore()
    peers = [yid(1), yid(2), yid(3), xid(1), xid(2), xid(3), other, zid(1), zid(2), zid(3)]
    peers += [(x * 2 + 1 - c, y * 4 + wrap(z + d)) for d in (1, 2, 3)]
    for dev in peers:
        pl.semaphore_signal(barrier, inc=1, device_id=dev, device_id_type=MESH)
    pl.semaphore_wait(barrier, len(peers))

    start(*[part(y_v, d=d, p=p) for d in ODD_FIRST for p in (0, 1)])
    start(part(z_p0, k=0), part(z_m0, k=0))

    def own(n):
        return [
            pltpu.make_async_copy(v1_in.at[:, quarter(y, n)], vk.at[0, y, z, :, pl.ds(0, n * 128)], ls.at[0]),
            pltpu.make_async_copy(v2_in.at[:, quarter(y, n)], vk.at[1, y, z, :, pl.ds(0, n * 128)], ls.at[1]),
            pltpu.make_async_copy(m_in.at[:, quarter(y, n)], mk.at[mrow(y), pl.ds(0, n * 128)], ls.at[2]),
            pltpu.make_async_copy(p_in.at[:, :, quarter(y, n)], pk.at[:, 0, zl, :, pl.ds(0, n * 128)], ls.at[3]),
        ]

    both(lambda n: [q.start() for q in own(n)] and None)

    def y_panel(h, ds=ODD_FIRST):
        start(*[part(y_p, d=d, h=h) for d in ds])

    def z_panel(h):
        arrived(*[part(y_p_in, d=d, h=h) for d in ODD_FIRST])
        start(part(z_p, h=h))

    start(*[part(y_m, d=d) for d in ODD_FIRST])
    y_panel(0)
    y_panel(1)

    arrived(*[part(y_v_in, d=d, p=p) for d in ODD_FIRST for p in (0, 1)])
    both(lambda n: [q.wait() for q in own(n)] and None)
    start(*[part(z_v, to=to, p=p) for p in (0, 1) for to in "mp"])
    start(part(z_m0, k=1))
    for p in (0, 1):
        arrived(part(z_v_in, to="m", p=p))
        start(part(z_vf, p=p))
    start(part(z_p0, k=1))

    first, second = pl.ds(0, 256), pl.ds(256, 256)

    def split_block(src, yy, base):
        @pl.loop(0, 2)
        def _(i):
            start_row = yy * 128 + i * 64
            to = pl.ds(pl.multiple_of(base + start_row, 64), 64)
            rh[to, :], rl[to, :] = split(src[pl.ds(pl.multiple_of(start_row, 64), 64), :])

    def product(h, lo, hi):
        for t in range(lo, hi):
            rows = pl.ds(t * 256, 256)
            ct[h, :, rows] = dot3((ph[h], plo[h]), (rh[rows, :], rl[rows, :]), NT)

    def landed(h):
        arrived(*([part(z_pe_in, e=e, h=h) for e in (1, 3, 2)] if h == 3 else [part(z_p_in, h=h)]),
                *([part(z_p0_in, k=0)] if h == 0 else [part(z_p0_in, k=1)] if h == 3 else []))

        @pl.loop(0, 4)
        def _(e):
            rows = pl.ds(pl.multiple_of(e * 64, 64), 64)
            ph[h, rows, :], plo[h, rows, :] = split(pk[h, e].reshape(64, W))

    def early(h):
        panel = pl.ds(pl.multiple_of(1024 + zl * 256, 256), 256)
        bt[h] = dot3((ph[h], plo[h]), (rh[panel, :], rl[panel, :]), NT)
        go(remote(("cb", h), bt.at[h, :, lanes(1 - c, 128)], cb.at[h], other))
        product(h, 0, 2)
        copy = remote(("cc", h), ct.at[h, :, pl.ds(0, 512)], cc.at[h], other)

        @pl.when(jnp.logical_not(home))
        def _():
            copy.start()

        away_sends.append(copy)

    def along_x(name, h, src, dst):
        out = []
        for f in ODD_FIRST:
            e = wrap(x + f - y + 4)
            out.append(remote((name, f, h), src.at[h, pl.ds(pl.multiple_of(e * 64, 64), 64)], dst.at[h, f - 1], xid(f)))
        return out

    def early_x(h):
        remote(("cb", h), cb.at[h], cb.at[h], other).wait_recv()
        kb[h] = bt[h, :, lanes(c, 128)] + cb[h]
        for q in along_x("xb", h, kb, bx):
            go(q)
        copies = along_x("xc", h, kc, cx)

        @pl.when(home)
        def _():
            remote(("cc", h), cc.at[h], cc.at[h], other).wait_recv()
            kc[h] = ct[h, :, pl.ds(0, 512)] + cc[h]
            for q in copies:
                q.start()

        home_sends.extend(copies)

    def late(h):
        product(h, 2, 4)
        copy = remote(("cc", h), ct.at[h, :, pl.ds(512, 512)], cc.at[h], other)

        @pl.when(home)
        def _():
            copy.start()

        home_sends.append(copy)

    def late_x(h):
        copies = along_x("xc", h, kc, cx)

        @pl.when(jnp.logical_not(home))
        def _():
            remote(("cc", h), cc.at[h], cc.at[h], other).wait_recv()
            kc[h] = ct[h, :, pl.ds(512, 512)] + cc[h]
            for q in copies:
                q.start()

        away_sends.extend(copies)

    mine = pl.ds(pl.multiple_of(wrap(x - y + 4) * 64, 64), 64)

    pair = lax.div(z, 2)
    b_slot = zl * 2 + c

    def b_copies(h):
        base = names("sbr", h, 0)
        for k in (1, 2, 3):
            names("sbr", h, k)
        return [pltpu.make_async_remote_copy(
            src_ref=sb.at[h], dst_ref=fb.at[h, :, lanes(b_slot, 128)], send_sem=ss.at[names("sbs", h, k)],
            recv_sem=rs.at[base + b_slot], device_id=(x * 2 + pair, y * 4 + wrap(z + k)), device_id_type=MESH)
            for k in range(4)]

    def finish_b(h):
        for f in ODD_FIRST:
            remote(("xb", f, h), bx.at[h, f - 1], bx.at[h, f - 1], xid(f)).wait_recv()
        sb[h] = (kb[h, mine, :] + bx[h, 0]) + (bx[h, 1] + bx[h, 2])
        copies = b_copies(h)
        for q in copies[1:]:
            go(q)

        @pl.when(home)
        def _():
            fb[h, :, lanes(b_slot, 128)] = sb[h]

        @pl.when(jnp.logical_not(home))
        def _():
            copies[0].start()

        away_sends.append(copies[0])

    def finish_c(h):
        for f in ODD_FIRST:
            remote(("xc", f, h), cx.at[h, f - 1], cx.at[h, f - 1], xid(f)).wait_recv()
        total = (kc[h, mine, :] + cx[h, 0]) + (cx[h, 1] + cx[h, 2])
        copy = remote(("sc", h), sc.at[h], fc.at[h], swap_mate)

        @pl.when(home)
        def _():
            fc[h] = total

        @pl.when(jnp.logical_not(home))
        def _():
            sc[h] = total
            copy.start()

        away_sends.append(copy)

    def final_b(h):
        for k in range(4):
            @pl.when(jnp.logical_not(jnp.logical_and(home, b_slot == k)))
            def _():
                ref = fb.at[h, :, pl.ds(k * 128, 128)]
                remote(("sbr", h, k), ref, ref, other).wait_recv()

        fbs = split(fb[h])
        for cols in (first, second):
            dt[h, :, cols] = dot3(fbs, (wh[cols, :], wl[cols, :]), NT)

    def final_c(h):
        @pl.when(jnp.logical_not(home))
        def _():
            remote(("sc", h), fc.at[h], fc.at[h], swap_mate).wait_recv()

        dt[h] = fc[h] - dt[h]
        for d in ODD_FIRST:
            go(remote(("cy", d, h), dt.at[h, :, lanes(wrap(y + d), 128)], cy.at[h, d - 1], yid(d)))

    def final(h):
        final_b(h)
        final_c(h)

    def done(h):
        for d in ODD_FIRST:
            remote(("cy", d, h), cy.at[h, d - 1], cy.at[h, d - 1], yid(d)).wait_recv()
        res = ((dt[h, :, lanes(y, 128)] + cy[h, 0]) + (cy[h, 1] + cy[h, 2])) / N
        out_c[pl.ds(h * 32, 32), :] = res[:32]
        out_c[pl.ds(128 + h * 32, 32), :] = res[32:]

    split_block(mk, y, 0)
    for e in (1, 3, 2):
        arrived(part(y_m_in, d=4 - e))
        start(part(z_m, e=e))
        split_block(mk, wrap(y + e), 0)
    arrived(*[part(z_v_in, to="p", p=p) for p in (0, 1)], *[part(z_vf_in, p=p) for p in (0, 1)])

    @pl.loop(0, 8)
    def _(i):
        p, yy = lax.div(i, 4), lax.rem(i, 4)
        rows = pl.ds(pl.multiple_of(1024 + i * 64, 64), 64)
        rh[rows, :], rl[rows, :] = split(vk[p, yy].reshape(64, W))

    v1s, v2s = pl.ds(1024, 256), pl.ds(1280, 256)
    gram = dot3((rh[v1s, :], rl[v1s, :]), (rh[v2s, :], rl[v2s, :]), NT)
    at[:, pl.ds(32, 8), first] = gram[:128].reshape(16, 8, 256)
    at[:, pl.ds(32, 8), second] = gram[128:].reshape(16, 8, 256)
    for t in (0, 1):
        rows = pl.ds(t * 256, 256)
        for j, cols in ((0, first), (1, second)):
            vrows = pl.ds(1024 + j * 256, 256)
            res = dot3((rh[rows, :], rl[rows, :]), (rh[vrows, :], rl[vrows, :]), NT)
            at[pl.ds(t * 8, 8), pl.ds(0, 32), cols] = res.reshape(8, 32, 256)

    core_sum = go(remote(("ac",), at.at[pl.ds((1 - c) * 8, 8)], ac, other))
    z_panel(0)
    core_sum.wait_recv()
    for k in range(8):
        at[c * 8 + k] = at[c * 8 + k] + ac[k]
    a0, b0 = c * 8, c * 8 + 4
    one = [go(remote(("ax", d), at.at[a0 + wrap(x + d)], ax.at[d - 1], xid(d))) for d in ODD_FIRST]
    one += [go(remote(("by", d), at.at[b0 + wrap(y + d)], by_.at[d - 1], yid(d))) for d in ODD_FIRST]
    y_panel(2)
    z_panel(1)
    for q in one:
        q.wait_recv()
    as_[0] = (at[a0 + x] + ax[0]) + (ax[1] + ax[2])
    as_[1] = (at[b0 + y] + by_[0]) + (by_[1] + by_[2])
    two = [go(remote(("ay", d), as_.at[0], ay.at[d - 1], yid(d))) for d in ODD_FIRST]
    two += [go(remote(("bx", d), as_.at[1], bx_.at[d - 1], xid(d))) for d in ODD_FIRST]

    y_panel(3, (1, 3))
    landed(0)
    early(0)
    early_x(0)
    z_panel(2)
    for q in two:
        q.wait_recv()
    af[a0 + x] = (as_[0] + ay[0]) + (ay[1] + ay[2])
    af[b0 + y] = (as_[1] + bx_[0]) + (bx_[1] + bx_[2])
    for d in ODD_FIRST:
        go(remote(("cx", d), af.at[a0 + x], af.at[a0 + x], xid(d)))
        go(remote(("dy", d), af.at[b0 + y], af.at[b0 + y], yid(d)))
    y_panel(3, (2,))
    landed(1)
    early(1)
    early_x(1)

    def modes_landed():
        arrived(part(z_m0_in, k=0), part(z_m0_in, k=1))
        split_block(mp, y, 512)
        for e in (1, 3, 2):
            rows = mrow(wrap(y + e))
            both(lambda n: remote(("zm", e), mp.at[rows, pl.ds(0, n * 128)], mp.at[rows, pl.ds(0, n * 128)],
                                  m_mate).wait_recv())
            split_block(mp, wrap(y + e), 512)

    def z_last(*es):
        arrived(*[part(y_p_in, d=4 - e, h=3) for e in es])
        start(*[part(z_pe, e=e, h=3) for e in es])

    z_last(1, 3)
    modes_landed()
    late(0)
    for d in ODD_FIRST:
        ref = af.at[a0 + wrap(x + 4 - d)]
        remote(("cx", d), ref, ref, xid(d)).wait_recv()
        ref = af.at[b0 + wrap(y + 4 - d)]
        remote(("dy", d), ref, ref, yid(d)).wait_recv()
    ref = af.at[pl.ds(c * 8, 8)]
    go(remote(("bc",), ref, ref, other))
    late_x(0)
    late(1)
    ref = af.at[pl.ds((1 - c) * 8, 8)]
    remote(("bc",), ref, ref, other).wait_recv()

    gram = jnp.concatenate([af[:, pl.ds(32, 8), first].reshape(128, 256),
                            af[:, pl.ds(32, 8), second].reshape(128, 256)], axis=0)
    gram2, f1s, f2s = split(gram), split(f1[...]), split(f2[...])
    for t in (0, 1):
        rows = pl.ds(t * 256, 256)
        a1 = af[pl.ds(t * 8, 8), pl.ds(0, 32), first].reshape(256, 256)
        a2 = af[pl.ds(t * 8, 8), pl.ds(0, 32), second].reshape(256, 256)
        w2 = split(dot3(split(a2), f2s, NT))
        wh[rows, second], wl[rows, second] = w2
        w1 = split(dot3(split(a1 - dot3(w2, gram2, NT)), f1s, NT))
        wh[rows, first], wl[rows, first] = w1

    vall = pl.ds(1024, 512)

    def move(d):
        rows = mrow(wrap(y + d))
        for k in range(2):
            cols = pl.ds(k * 512, 512)
            mv[rows, cols] = mk[rows, cols] - dot3((wh[rows, :], wl[rows, :]), (rh[vall, cols], rl[vall, cols]), NN)

    def own_r(n):
        return pltpu.make_async_copy(mv.at[mrow(y), pl.ds(0, n * 128)], out_m.at[:, quarter(y, n)], ls.at[4])

    z_last(2)
    late_x(1)
    move(1)
    start(part(y_r, d=1, half=0))
    move(3)
    start(part(y_r, d=3, half=0))
    landed(2)
    early(2)
    move(2)
    start(part(y_r, d=2, half=0))
    early_x(2)
    late(2)
    move(0)
    both(lambda n: own_r(n).start())
    late_x(2)
    start(*[part(y_r, d=d, half=1) for d in ODD_FIRST])
    finish_b(0)
    finish_b(1)
    landed(3)
    late(3)
    early(3)
    late_x(3)
    early_x(3)
    finish_c(0)
    finish_c(1)
    finish_b(2)
    final(0)
    finish_c(2)
    final(1)
    finish_b(3)
    finish_c(3)
    final(2)
    final_b(3)
    final_c(3)
    drain()
    done(0)
    done(1)
    done(2)
    done(3)

    arrived(*[part(y_r_in, d=d, half=half) for half in (0, 1) for d in ODD_FIRST])
    both(lambda n: own_r(n).wait())
    assert len(names.ids) <= SEMS, len(names.ids)


SEMS = 192


def place(m_ref, t_ref, m_out, c_out, m_buf, t_buf, c_buf, come, go):
    rows = [pl.ds(i * 16, 16) for i in range(8)]
    reads = [pltpu.make_async_copy(t_ref, t_buf, come.at[8])]
    reads += [pltpu.make_async_copy(m_ref.at[q], m_buf.at[q], come.at[i]) for i, q in enumerate(rows)]
    writes = [pltpu.make_async_copy(c_buf, c_out, go.at[8])]
    writes += [pltpu.make_async_copy(m_buf.at[q], m_out.at[q], go.at[i]) for i, q in enumerate(rows)]
    for copy in reads:
        copy.start()
    reads[0].wait()
    c_buf[...] = t_buf[...].T
    writes[0].start()
    for come_in, go_out in zip(reads[1:], writes[1:]):
        come_in.wait()
        go_out.start()
    for copy in writes:
        copy.wait()


def shards(modes, prev_modes, first_vectors, first_factor, second_vectors, second_factor):
    any_, vmem = pl.BlockSpec(memory_space=pl.ANY), pl.BlockSpec(memory_space=pltpu.VMEM)
    V = pltpu.VMEM
    dma = pltpu.SemaphoreType.DMA
    moved, turned = pl.pallas_call(
        kernel,
        out_shape=(jax.ShapeDtypeStruct((128, 3840), F32), jax.ShapeDtypeStruct((256, 128), F32)),
        in_specs=[any_, any_, any_, any_, vmem, vmem],
        out_specs=(any_, vmem),
        scratch_shapes=[
            V((512, W), F32), V((512, W), F32), V((512, W), F32), V((4, 4, 2, 32, W), F32), V((2, 4, 4, 16, W), F32),
            V((1536, W), BF16), V((1536, W), BF16), V((4, 256, W), BF16), V((4, 256, W), BF16),
            V((16, 40, 512), F32), V((8, 40, 512), F32), V((3, 40, 512), F32), V((3, 40, 512), F32),
            V((3, 40, 512), F32), V((3, 40, 512), F32), V((2, 40, 512), F32), V((16, 40, 512), F32),
            V((512, 512), BF16), V((512, 512), BF16),
            V((4, 256, 1024), F32), V((4, 256, 256), F32), V((4, 256, 512), F32), V((4, 256, 128), F32),
            V((4, 256, 512), F32), V((4, 256, 128), F32), V((4, 3, 64, 512), F32), V((4, 3, 64, 128), F32),
            V((4, 64, 512), F32), V((4, 64, 128), F32), V((4, 64, 512), F32), V((4, 64, 512), F32),
            V((4, 64, 512), F32), V((4, 3, 64, 128), F32),
            dma((SEMS,)), dma((SEMS,)), dma((5,)),
        ],
        compiler_params=pltpu.CompilerParams(
            collective_id=0, has_side_effects=True, vmem_limit_bytes=60 * 2**20),
        name="reflect_and_correlate",
    )(modes, prev_modes.reshape(4, 32, 3840), first_vectors, second_vectors, first_factor, second_factor)
    return pl.pallas_call(
        place,
        out_shape=(jax.ShapeDtypeStruct((128, 3840), F32), jax.ShapeDtypeStruct((128, 256), F32)),
        in_specs=[any_, any_],
        out_specs=(any_, any_),
        scratch_shapes=[V((128, 3840), F32), V((256, 128), F32), V((128, 256), F32), dma((9,)), dma((9,))],
        compiler_params=pltpu.CompilerParams(vmem_limit_bytes=60 * 2**20),
        name="place",
    )(moved, turned)


def solution(mesh):
    in_specs = (P("col", "row"), P("col", "row"), P("col", "row"), P(), P("col", "row"), P())
    out_specs = (P("col", "row"), P("col", "row"))
    return jax.shard_map(shards, mesh=mesh, in_specs=in_specs, out_specs=out_specs, check_vma=False)
```
